256 devices in a mesh: walk: 16 (over x, z_hi), chol: 16 (over y, z_lo, core).
Axes of the slice: x: 4, y: 4, z: 8 (z_hi: 4, z_lo: 2; z = z_hi * 2 + z_lo), core: 2. Of those that a mesh axis runs over, the one named last changes fastest.
Arguments:
- walkers: float32 [256, 640, 128], P(('walk', 'chol')), may hold values from -6 to 6
- intersection_inverse: float32 [256, 128, 128], P(('walk', 'chol')), may hold values from -0.2 to 1.2
- aux_draws: float32 [256, 3072], P(None, 'chol'), may hold values from -6 to 6
- chol_half: bfloat16 [3072, 640, 128], P('chol', 'walk'), may hold values from -0.01953125 to 0.01953125
- chol_full: bfloat16 [3072, 640, 640], P('chol', 'walk'), may hold values from -0.00390625 to 0.00390625
Outputs:
- new_walkers: float32 [256, 640, 128], P(('walk', 'chol'))
- aux_field: float32 [256, 3072], P(None, 'chol')
The draws below stay inside these ranges and needn't reach their ends.
All inputs are finite; a program needn't handle non-finite values.
Results may differ from the reference program's by a relative error of at most 0.04.
Values may be sent and summed in bfloat16 or wider, within the bound.
A program may use at most 128 MiB of HBM per device.

```python
import math
import jax
import jax.numpy as jnp
from jax import lax

ORBITALS = 640
ELECTRONS = 128
NCHOL = 3072
WALKERS = 256
N_CHOL = 16


def draw_intersection_inverse(key, part):
    key = jax.random.fold_in(key, 7)
    shape = (WALKERS, ELECTRONS, ELECTRONS)
    noise = jnp.clip(jax.random.normal(key, shape, jnp.float32), -4.0, 4.0)
    identity = jnp.eye(ELECTRONS, dtype=jnp.float32)
    matrix = identity[None, :, :] + 0.5 / math.sqrt(ELECTRONS) * noise
    return jnp.clip(matrix, -0.2, 1.2)


def strengthened(values, stream_key, source, target, shards_of, factor):
    owner, partner = [(jnp.arange(values.shape[position]) // (values.shape[position] // shards_of)).reshape([-1 if axis == position else 1 for axis in range(values.ndim)]) for position in (source, target)]
    chosen = jax.random.permutation(stream_key, shards_of)[partner]
    strong = (owner == chosen) | (owner == (partner + shards_of // 2) % shards_of)
    return jnp.where(strong, factor * values, values)


def block_levels(stream_key, shape, pieces, smallest, high):
    level = 1.0
    for axis_at, parts in pieces:
        heights = jax.random.uniform(jax.random.fold_in(jax.random.fold_in(stream_key, 6), axis_at), (parts,), jnp.float32, smallest / len(pieces), high / len(pieces))
        level = level * jnp.repeat(jnp.exp(heights), shape[axis_at] // parts).reshape((-1,) + (1,) * (len(shape) - 1 - axis_at))
    return level


def gaussian(own_key, extent, width, limit, pieces=(), kind=jnp.bfloat16):
    entries = width * jax.random.normal(own_key, extent, jnp.float32)
    if pieces:
        entries = entries * block_levels(own_key, extent, pieces, -0.22, 0.18)
    return jnp.clip(entries, -limit, limit).astype(kind)


def bell_draw_with(own_key, shape, spread, limit, pieces, heavy, kind=jnp.bfloat16):
    result = spread * jax.random.normal(own_key, shape, jnp.float32)
    if pieces:
        result = result * block_levels(own_key, shape, pieces, -0.22, 0.18)
    return jnp.clip(strengthened(result, jax.random.fold_in(own_key, 3), *heavy), -limit, limit).astype(kind)


def setup_inputs(seed: int = 0) -> dict:
    streams_of = jax.random.split(jax.random.key(seed), 6)
    walkers = gaussian(streams_of[0], (WALKERS, ORBITALS, ELECTRONS), 1.0, 6.0, ((0, 256),), jnp.float32)
    intersection_inverse = draw_intersection_inverse(jax.random.fold_in(streams_of[5], 71), 0)
    aux_draws = bell_draw_with(streams_of[2], (WALKERS, NCHOL), 1.0, 6.0, ((1, 16),), (1, 0, 16, 2.0), jnp.float32)
    chol_half = gaussian(streams_of[3], (NCHOL, ORBITALS, ELECTRONS), (ORBITALS * ELECTRONS) ** -0.5, 0.01953125, ((0, 16), (1, 16)))
    chol_full = gaussian(streams_of[4], (NCHOL, ORBITALS, ORBITALS), (NCHOL * ORBITALS) ** -0.5, 0.00390625, ((0, 16), (1, 16)))
    return {"walkers": walkers, "intersection_inverse": intersection_inverse, "aux_draws": aux_draws, "chol_half": chol_half, "chol_full": chol_full}


def reference(walkers, intersection_inverse, aux_draws, chol_half, chol_full):
    green_half = jnp.einsum("wpj,wji->wpi", walkers, intersection_inverse, precision=lax.Precision.HIGHEST).astype(jnp.bfloat16)
    half_flat = chol_half.reshape(NCHOL, ORBITALS * ELECTRONS)
    force_bias = jnp.dot(green_half.reshape(WALKERS, ORBITALS * ELECTRONS), half_flat.T, preferred_element_type=jnp.float32)
    aux_field = aux_draws - force_bias
    field_low = aux_field.astype(jnp.bfloat16)
    group_size = NCHOL // N_CHOL
    full_flat = chol_full.reshape(NCHOL, ORBITALS * ORBITALS)

    def add_group(group, summed):
        offset = (group * group_size).astype(jnp.int32)
        field_block = lax.dynamic_slice_in_dim(field_low, offset, group_size, 1)
        vector_block = lax.dynamic_slice_in_dim(full_flat, offset, group_size, 0)
        partial_value = jnp.dot(field_block, vector_block, preferred_element_type=jnp.float32).astype(jnp.bfloat16)
        return summed + partial_value.astype(jnp.float32)

    summed = lax.fori_loop(0, N_CHOL, add_group, jnp.zeros((WALKERS, ORBITALS * ORBITALS), jnp.float32))
    operator = summed.astype(jnp.bfloat16).reshape(WALKERS, ORBITALS, ORBITALS)
    operator_wide = lax.optimization_barrier(operator).astype(jnp.float32)
    taylor_term = walkers
    new_walkers = walkers
    for degree in range(1, 5):
        term_low = lax.optimization_barrier(taylor_term.astype(jnp.bfloat16))
        taylor_term = jnp.einsum("wrs,wsi->wri", operator_wide, term_low.astype(jnp.float32)) / degree
        new_walkers = new_walkers + taylor_term
    return new_walkers, aux_field
```

```python
import jax
import jax.numpy as jnp
from jax import lax
from jax.sharding import PartitionSpec as P


def body(walkers, intersection_inverse, aux_draws, chol_half, chol_full):
    walk_size = lax.axis_size("walk")
    chol_size = lax.axis_size("chol")
    per_device, orbitals, electrons = walkers.shape
    slab_rows = orbitals // walk_size
    local_vectors = chol_half.shape[0]
    group_walkers = walk_size * per_device
    total_walkers = group_walkers * chol_size
    green_half = jnp.einsum(
        "wpj,wji->wpi", walkers, intersection_inverse, precision=lax.Precision.HIGHEST
    ).astype(jnp.bfloat16)
    green_slab = lax.all_to_all(green_half, "walk", split_axis=1, concat_axis=0, tiled=True)
    half_flat = chol_half.reshape(local_vectors, slab_rows * electrons)
    piece = lax.all_gather(green_slab, "chol", axis=0, tiled=True)
    flat_piece = piece.reshape(piece.shape[0], slab_rows * electrons)
    partial_bias = lax.dot_general(
        flat_piece, half_flat, (((1,), (1,)), ((), ())), preferred_element_type=jnp.float32
    )
    parts = partial_bias.astype(jnp.bfloat16).reshape(walk_size, -1, local_vectors)
    parts = lax.all_to_all(parts, "walk", split_axis=0, concat_axis=0, tiled=True)
    own_bias = jnp.sum(parts.astype(jnp.float32), axis=0).astype(jnp.bfloat16)
    force_bias = lax.all_gather(own_bias, "walk", axis=0, tiled=True).astype(jnp.float32)
    draws_sorted = aux_draws.reshape(walk_size, chol_size, per_device, local_vectors)
    draws_sorted = draws_sorted.transpose(1, 0, 2, 3).reshape(total_walkers, local_vectors)
    field_sorted = draws_sorted - force_bias
    aux_field = field_sorted.reshape(chol_size, walk_size, per_device, local_vectors)
    aux_field = aux_field.transpose(1, 0, 2, 3).reshape(total_walkers, local_vectors)
    field_low = field_sorted.astype(jnp.bfloat16)
    full_flat = chol_full.reshape(local_vectors, slab_rows * orbitals)
    summed = lax.psum_scatter(
        jnp.dot(field_low, full_flat, preferred_element_type=jnp.float32).astype(jnp.bfloat16),
        "chol",
        scatter_dimension=0,
        tiled=True,
    )
    operator = summed.reshape(group_walkers, slab_rows, orbitals)
    operator = lax.all_to_all(operator, "walk", split_axis=0, concat_axis=1, tiled=True)
    taylor_term = walkers
    new_walkers = walkers
    for degree in range(1, 5):
        taylor_term = (
            jnp.einsum(
                "wrs,wsi->wri",
                operator,
                taylor_term.astype(jnp.bfloat16),
                preferred_element_type=jnp.float32,
            )
            / degree
        )
        new_walkers = new_walkers + taylor_term
    return (new_walkers, aux_field)


def solution(mesh):
    placed = (
        P(("walk", "chol"), None, None),
        P(("walk", "chol"), None, None),
        P(None, "chol"),
        P("chol", "walk", None),
        P("chol", "walk", None),
    )
    return jax.shard_map(
        body,
        mesh=mesh,
        in_specs=placed,
        out_specs=(P(("walk", "chol"), None, None), P(None, "chol")),
        check_vma=False,
    )
```

```python
import functools

import jax
import jax.numpy as jnp
from jax import lax
from jax.experimental import pallas as pl
from jax.experimental.pallas import tpu as pltpu
from jax.sharding import PartitionSpec as P

MESH = pl.DeviceIdType.MESH
BF16 = jnp.bfloat16
F32 = jnp.float32
ANY = pl.BlockSpec(memory_space=pl.ANY)
VMEM = pl.BlockSpec(memory_space=pltpu.VMEM)


def place():
    a = lax.axis_index("walk")
    b = lax.axis_index("chol")
    return a, b // 4, (b // 2) % 2, b % 2


def at(a, y, z, c):
    return (a, y * 4 + z * 2 + c)


def remote(src, dst, send, recv, target):
    return pltpu.make_async_remote_copy(
        src_ref=src, dst_ref=dst, send_sem=send, recv_sem=recv, device_id=target, device_id_type=MESH
    )


def greet(target):
    pl.semaphore_signal(pltpu.get_barrier_semaphore(), inc=1, device_id=target, device_id_type=MESH)


def field_kernel(
    walkers, inverse, draws, half, full,
    aux_out, field_out, ct_out,
    wv, iv, dv, hv, fv, gsend, g1, blocks, ht, ct, pb, bin_, ball, field,
    in_sem, ct_sem, ct_send, ct_recv, a_send, a_recv, g_send, g_recv, p_send, p_recv, b_send, b_recv,
    f_send, f_recv,
):
    a, y, z, c = place()
    up, down = (y + 1) % 4, (y + 3) % 4
    sibling = at(a, y, z, 1 - c)
    loads = [
        pltpu.make_async_copy(walkers, wv, in_sem.at[0]),
        pltpu.make_async_copy(inverse, iv, in_sem.at[1]),
        pltpu.make_async_copy(half, hv, in_sem.at[2]),
        pltpu.make_async_copy(full, fv, in_sem.at[3]),
        pltpu.make_async_copy(draws, dv, in_sem.at[4]),
    ]
    for load in loads:
        load.start()

    def greet_walk(d, _):
        greet(at((a + d) % 16, y, z, c))
        return 0

    lax.fori_loop(1, 16, greet_walk, 0)
    greet(at(a, up, z, c))
    greet(at(a, down, z, c))
    greet(at(a, y, 1 - z, c))
    greet(sibling)

    loads[0].wait()
    loads[1].wait()
    green = jnp.dot(
        wv[0], iv[0], precision=lax.Precision.HIGHEST, preferred_element_type=F32
    ).astype(BF16)
    gsend[...] = green.reshape(16, 40, 128)
    pl.semaphore_wait(pltpu.get_barrier_semaphore(), 19)

    def green_copy(d):
        to = (a + d) % 16
        return remote(gsend.at[to], g1.at[a], a_send.at[d], a_recv.at[d], at(to, y, z, c))

    def start_green(d, _):
        green_copy(d).start()
        return 0

    lax.fori_loop(1, 16, start_green, 0)
    g1[a] = gsend[a]

    loads[2].wait()

    def turn_half(i, _):
        n0 = pl.multiple_of(i * 16, 16)
        ht[:, pl.ds(n0, 16), :] = jnp.swapaxes(hv[pl.ds(n0, 16)], 0, 1)
        return 0

    lax.fori_loop(0, 12, turn_half, 0)

    def wait_green(d, _):
        green_copy(d).wait()
        return 0

    lax.fori_loop(1, 16, wait_green, 0)

    def slot(yy, zz):
        return c * 8 + yy * 2 + zz

    own = slot(y, z)
    blocks[own] = jnp.swapaxes(g1[...], 0, 1)

    first, second = pl.ds(0, 20), pl.ds(20, 20)

    def spread(index, ref, target):
        return remote(ref, ref, g_send.at[index], g_recv.at[index], target)

    to_up, to_down, to_z = at(a, up, z, c), at(a, down, z, c), at(a, y, 1 - z, c)
    far = (y + 2) % 4
    block = lambda yy, zz: blocks.at[slot(yy, zz)]
    copies = [
        spread(0, block(y, z), to_up),
        spread(1, block(y, z), to_down),
        spread(2, block(y, z), to_z),
        spread(3, block(y, z), sibling),
        spread(4, block(y, 1 - z), to_up),
        spread(5, block(y, 1 - z), to_down),
        spread(6, block(y, 1 - z), sibling),
        spread(7, block(down, z).at[first], to_up),
        spread(8, block(down, z), sibling),
        spread(9, block(up, z).at[second], to_down),
        spread(10, block(up, z), sibling),
        spread(11, block(down, 1 - z).at[first], to_up),
        spread(12, block(down, 1 - z), sibling),
        spread(13, block(up, 1 - z).at[second], to_down),
        spread(14, block(up, 1 - z), sibling),
        spread(15, block(far, z), sibling),
        spread(16, block(far, 1 - z), sibling),
    ]
    for index in (0, 1, 2, 3):
        copies[index].start()

    loads[3].wait()

    def turn_full(group):
        def turn(i, _):
            n0 = pl.multiple_of(i * 16, 16)
            ct[group, :, pl.ds(n0, 16), :] = jnp.swapaxes(
                fv[pl.ds(n0, 16), group * 8 : group * 8 + 8, :], 0, 1
            )
            return 0

        lax.fori_loop(0, 12, turn, 0)

    def keep(i):
        group = 4 if i == 2 else 2 * c + i
        return pltpu.make_async_copy(ct.at[group], ct_out.at[i, :, c], ct_sem.at[i])

    def give(i):
        group = 4 if i == 2 else 2 * (1 - c) + i
        return remote(ct.at[group], ct_out.at[i, :, c], ct_send.at[i], ct_recv.at[i], sibling)

    turn_full(0)
    turn_full(1)
    copies[2].wait_recv()
    for index in (4, 5, 6):
        copies[index].start()
    copies[0].wait_recv()
    copies[1].wait_recv()
    for index in (7, 9, 8, 10):
        copies[index].start()
    turn_full(2)
    turn_full(3)
    for i in (0, 1):
        keep(i).start()
        give(i).start()
    copies[4].wait_recv()
    copies[5].wait_recv()
    for index in (11, 13, 12, 14):
        copies[index].start()
    turn_full(4)
    keep(2).start()
    give(2).start()
    copies[7].wait_recv()
    copies[9].wait_recv()
    copies[15].start()
    copies[11].wait_recv()
    copies[13].wait_recv()
    copies[16].start()
    loads[4].wait()
    draws_by_slot = jnp.swapaxes(dv[...], 0, 1).reshape(8, 2, 16, 192)
    for index in (3, 6, 8, 10, 12, 14, 15, 16):
        copies[index].wait_recv()

    def bias_step(i, acc):
        p0 = i * 8
        left = jnp.concatenate([blocks[:, p0 + q].reshape(256, 128) for q in range(8)], axis=1)
        right = jnp.concatenate([ht[p0 + q] for q in range(8)], axis=1)
        return acc + lax.dot_general(
            left, right, (((1,), (1,)), ((), ())), preferred_element_type=F32
        )

    partial = lax.fori_loop(0, 5, bias_step, jnp.zeros((256, 192), F32))
    pb[...] = partial.astype(BF16).reshape(16, 16, 192)

    def part_copy(d):
        to = (a + d) % 16
        return remote(pb.at[to], bin_.at[a], p_send.at[d], p_recv.at[d], at(to, y, z, c))

    def start_part(d, _):
        part_copy(d).start()
        return 0

    def wait_part(d, _):
        part_copy(d).wait()
        return 0

    lax.fori_loop(1, 16, start_part, 0)
    bin_[a] = pb[a]
    lax.fori_loop(1, 16, wait_part, 0)
    ball[a] = jnp.sum(bin_[...].astype(F32), axis=0).astype(BF16)

    def bias_copy(d):
        to = (a + d) % 16
        return remote(ball.at[a], ball.at[a], b_send.at[d], b_recv.at[d], at(to, y, z, c))

    def bias_from(d):
        there = (a + 16 - d) % 16
        return remote(ball.at[there], ball.at[there], b_send.at[d], b_recv.at[d], at(there, y, z, c))

    def start_bias(d, _):
        bias_copy(d).start()
        return 0

    def wait_bias(d, _):
        bias_copy(d).wait_send()
        bias_from(d).wait_recv()
        return 0

    lax.fori_loop(1, 16, start_bias, 0)
    lax.fori_loop(1, 16, wait_bias, 0)
    bias = jnp.swapaxes(ball[...].astype(F32).reshape(2, 8, 16, 192), 0, 1)
    shifted = draws_by_slot - bias
    for owner in range(2):
        field[c, owner] = shifted[:, owner].astype(BF16)
    field_copy = remote(field.at[c], field.at[c], f_send, f_recv, sibling)
    field_copy.start()
    aux_out[...] = jnp.swapaxes(shifted.reshape(16, 16, 192), 0, 1)
    for copy in copies:
        copy.wait_send()
    for i in range(3):
        keep(i).wait()
        give(i).wait()
    field_copy.wait()
    field_out[...] = field[...]


def propagate_kernel(
    walkers, field, ct_in,
    out,
    ct, part, pass_up, pass_down, from_down, from_up, z_out, from_z, turned, operator,
    ct_sem, s_up, r_up, s_down, r_down, z_send, z_recv, o_send, o_recv,
):
    a, y, z, c = place()
    up, down, far = (y + 1) % 4, (y + 3) % 4, (y + 2) % 4
    to_up, to_down, to_z = at(a, up, z, c), at(a, down, z, c), at(a, y, 1 - z, c)
    loads = [pltpu.make_async_copy(ct_in.at[i], ct.at[i], ct_sem.at[i]) for i in range(3)]
    for load in loads:
        load.start()

    def greet_walk(d, _):
        greet(at((a + d) % 16, y, z, c))
        greet(at((a + d) % 16, y, z, 1 - c))
        return 0

    lax.fori_loop(1, 16, greet_walk, 0)
    greet(to_up)
    greet(to_down)
    greet(to_z)
    greet(at(a, y, z, 1 - c))

    low, high = pl.ds(0, 4), pl.ds(4, 4)

    def owner_of(k):
        return c if k == 4 else k % 2

    def group_of(k):
        return 4 if k == 4 else 2 * c + k // 2

    def multiply(k):
        if k % 2 == 0:
            loads[k // 2].wait()
        owner = owner_of(k)
        left = [field[s, owner].reshape(128, 192) for s in range(2)]

        def row(r, _):
            value = jnp.dot(left[0], ct[k // 2, r, 0], preferred_element_type=F32)
            value = value + jnp.dot(left[1], ct[k // 2, r, 1], preferred_element_type=F32)
            part[k, :, :, r] = value.astype(BF16).reshape(4, 2, 16, 640)
            return 0

        lax.fori_loop(0, 8, row, 0)

    def sends(k):
        return (
            remote(part.at[k, far, :, low], pass_up.at[k], s_up.at[k, 0], r_up.at[k, 0], to_up),
            remote(part.at[k, far, :, high], pass_down.at[k], s_down.at[k, 0], r_down.at[k, 0], to_down),
            remote(part.at[k, up, :, high], from_down.at[k, :, high], s_up.at[k, 1], r_up.at[k, 1], to_up),
            remote(part.at[k, down, :, low], from_up.at[k, :, low], s_down.at[k, 1], r_down.at[k, 1], to_down),
            remote(pass_up.at[k], from_down.at[k, :, low], s_up.at[k, 2], r_up.at[k, 2], to_up),
            remote(pass_down.at[k], from_up.at[k, :, high], s_down.at[k, 2], r_down.at[k, 2], to_down),
        )

    def begin(k):
        for copy in sends(k)[:4]:
            copy.start()

    def pass_on(k):
        copies = sends(k)
        copies[0].wait_recv()
        pass_up[k] = (pass_up[k].astype(F32) + part[k, up, :, 0:4].astype(F32)).astype(BF16)
        copies[4].start()
        copies[1].wait_recv()
        pass_down[k] = (pass_down[k].astype(F32) + part[k, down, :, 4:8].astype(F32)).astype(BF16)
        copies[5].start()

    def z_copy(k):
        return remote(z_out.at[k], from_z.at[k], z_send.at[k], z_recv.at[k], to_z)

    def over_z(k):
        for copy in sends(k)[2:]:
            copy.wait_recv()
        other = 1 - z
        total = part[k, y, other].astype(F32) + from_down[k, other].astype(F32)
        z_out[k] = (total + from_up[k, other].astype(F32)).astype(BF16)
        z_copy(k).start()

    def owner_copy(k, d):
        to = (a + d) % 16
        return remote(
            turned.at[k, to], operator.at[a, group_of(k)],
            o_send.at[k, d], o_recv.at[group_of(k), d], at(to, y, z, owner_of(k)),
        )

    def deliver(k):
        z_copy(k).wait_recv()
        total = part[k, y, z].astype(F32) + from_down[k, z].astype(F32)
        total = total + from_up[k, z].astype(F32) + from_z[k].astype(F32)
        turned[k] = jnp.swapaxes(total, 0, 1).astype(BF16)

        def start(d, _):
            owner_copy(k, d).start()
            return 0

        lax.fori_loop(1, 16, start, 0)
        if k == 4:
            operator[a, 4] = turned[k, a]
        else:

            @pl.when(c == k % 2)
            def _():
                operator[a, group_of(k)] = turned[k, a]

            @pl.when(c != k % 2)
            def _():
                owner_copy(k, 0).start()

    multiply(0)
    pl.semaphore_wait(pltpu.get_barrier_semaphore(), 34)
    begin(0)
    multiply(1)
    begin(1)
    for k in range(5):
        pass_on(k)
        if k + 2 < 5:
            multiply(k + 2)
            begin(k + 2)
        if k >= 1:
            over_z(k - 1)
        if k >= 2:
            deliver(k - 2)
    over_z(4)
    deliver(3)
    deliver(4)

    def arrival(group, d):
        return remote(
            turned.at[0, 0], operator.at[0, group], o_send.at[0, 0], o_recv.at[group, d], at(a, y, z, 1 - c)
        )

    for group in range(5):

        def wait_for(d, _, group=group):
            arrival(group, d).wait_recv()
            return 0

        lax.fori_loop(1, 16, wait_for, 0)
        if group < 4:

            @pl.when(c != group // 2)
            def _(group=group):
                arrival(group, 0).wait_recv()

    matrix = operator[...].reshape(640, 640)
    term = walkers[0]
    total = term
    for degree in range(1, 5):
        term = jnp.dot(matrix, term.astype(BF16), preferred_element_type=F32) * (1.0 / degree)
        total = total + term
    out[0] = total

    for k in range(5):
        for copy in sends(k):
            copy.wait_send()
        z_copy(k).wait_send()

        def wait_sent(d, _, k=k):
            owner_copy(k, d).wait_send()
            return 0

        lax.fori_loop(1, 16, wait_sent, 0)
        if k < 4:

            @pl.when(c != k % 2)
            def _(k=k):
                owner_copy(k, 0).wait_send()


def shape(*dims, dtype=BF16):
    return jax.ShapeDtypeStruct(dims, dtype)


def dma(*dims):
    return pltpu.SemaphoreType.DMA(dims)


def body(walkers, intersection_inverse, aux_draws, chol_half, chol_full):
    aux, field, ct = pl.pallas_call(
        field_kernel,
        out_shape=(
            shape(16, 16, 192, dtype=F32),
            shape(2, 2, 8, 16, 192),
            shape(3, 8, 2, 192, 640),
        ),
        in_specs=[ANY] * 5,
        out_specs=(VMEM, VMEM, ANY),
        scratch_shapes=[
            pltpu.VMEM((1, 640, 128), F32),
            pltpu.VMEM((1, 128, 128), F32),
            pltpu.VMEM((16, 16, 192), F32),
            pltpu.VMEM((192, 40, 128), BF16),
            pltpu.VMEM((192, 40, 640), BF16),
            pltpu.VMEM((16, 40, 128), BF16),
            pltpu.VMEM((16, 40, 128), BF16),
            pltpu.VMEM((16, 40, 16, 128), BF16),
            pltpu.VMEM((40, 192, 128), BF16),
            pltpu.VMEM((5, 8, 192, 640), BF16),
            pltpu.VMEM((16, 16, 192), BF16),
            pltpu.VMEM((16, 16, 192), BF16),
            pltpu.VMEM((16, 16, 192), BF16),
            pltpu.VMEM((2, 2, 8, 16, 192), BF16),
            dma(5), dma(3), dma(3), dma(3), dma(16), dma(16), dma(17), dma(17),
            dma(16), dma(16), dma(16), dma(16), dma(), dma(),
        ],
        compiler_params=pltpu.CompilerParams(
            collective_id=0, has_side_effects=True, vmem_limit_bytes=56 * 2**20
        ),
        name="field",
    )(walkers, intersection_inverse, aux_draws.reshape(16, 16, 192), chol_half, chol_full)
    new_walkers = pl.pallas_call(
        propagate_kernel,
        out_shape=shape(1, 640, 128, dtype=F32),
        in_specs=[VMEM, VMEM, ANY],
        out_specs=VMEM,
        scratch_shapes=[
            pltpu.VMEM((3, 8, 2, 192, 640), BF16),
            pltpu.VMEM((5, 4, 2, 8, 16, 640), BF16),
            pltpu.VMEM((5, 2, 4, 16, 640), BF16),
            pltpu.VMEM((5, 2, 4, 16, 640), BF16),
            pltpu.VMEM((5, 2, 8, 16, 640), BF16),
            pltpu.VMEM((5, 2, 8, 16, 640), BF16),
            pltpu.VMEM((5, 8, 16, 640), BF16),
            pltpu.VMEM((5, 8, 16, 640), BF16),
            pltpu.VMEM((5, 16, 8, 640), BF16),
            pltpu.VMEM((16, 5, 8, 640), BF16),
            dma(3), dma(5, 3), dma(5, 3), dma(5, 3), dma(5, 3), dma(5), dma(5), dma(5, 16), dma(5, 16),
        ],
        compiler_params=pltpu.CompilerParams(
            collective_id=1, has_side_effects=True, vmem_limit_bytes=56 * 2**20
        ),
        name="propagate",
    )(walkers, field, ct)
    return new_walkers, aux.reshape(256, 192)


def solution(mesh):
    placed = (
        P(("walk", "chol"), None, None),
        P(("walk", "chol"), None, None),
        P(None, "chol"),
        P("chol", "walk", None),
        P("chol", "walk", None),
    )
    return jax.shard_map(
        body,
        mesh=mesh,
        in_specs=placed,
        out_specs=(P(("walk", "chol"), None, None), P(None, "chol")),
        check_vma=False,
    )
```

```python
import jax
import jax.numpy as jnp
from jax import lax
from jax.experimental import pallas as pl
from jax.experimental.pallas import tpu as pltpu
from jax.sharding import PartitionSpec as P

MESH = pl.DeviceIdType.MESH
BF16 = jnp.bfloat16
F32 = jnp.float32
ANY = pl.BlockSpec(memory_space=pl.ANY)
VMEM = pl.BlockSpec(memory_space=pltpu.VMEM)


def place():
    a = lax.axis_index("walk")
    b = lax.axis_index("chol")
    return a, b // 4, (b // 2) % 2, b % 2


def at(a, y, z, c):
    return (a, y * 4 + z * 2 + c)


def remote(src, dst, send, recv, target):
    return pltpu.make_async_remote_copy(
        src_ref=src, dst_ref=dst, send_sem=send, recv_sem=recv, device_id=target, device_id_type=MESH
    )


def greet(target):
    pl.semaphore_signal(pltpu.get_barrier_semaphore(), inc=1, device_id=target, device_id_type=MESH)


def kernel(
    walkers, inverse, draws, half, full,
    out, aux_out,
    wv, iv, dv, hv, fv, gsend, g1, blocks, ht, ct, given, pb, parts_in, ball, field,
    part, pass_up, pass_down, from_down, from_up, z_out, from_z,
    zin, zsum, z_pass_up, z_pass_down, z_from_down, z_from_up, turned, operator,
    in_sem, ct_send, ct_recv, a_send, a_recv, g_send, g_recv, p_send, p_recv, b_send, b_recv,
    f_send, f_recv, s_up, r_up, s_down, r_down, z_send, z_recv, o_send, o_recv,
):
    a, y, z, c = place()
    up, down, far = (y + 1) % 4, (y + 3) % 4, (y + 2) % 4
    to_up, to_down, to_z = at(a, up, z, c), at(a, down, z, c), at(a, y, 1 - z, c)
    sibling = at(a, y, z, 1 - c)

    def load(index):
        pair = ((walkers, wv), (inverse, iv), (half, hv), (full, fv), (draws, dv))[index]
        return pltpu.make_async_copy(pair[0], pair[1], in_sem.at[index])

    for index in range(5):
        load(index).start()

    def greet_walk(d, _):
        greet(at((a + d) % 16, y, z, c))
        greet(at((a + d) % 16, y, z, 1 - c))
        return 0

    lax.fori_loop(1, 16, greet_walk, 0)
    for target in (to_up, to_down, to_z, sibling):
        greet(target)

    load(0).wait()
    load(1).wait()
    green = jnp.dot(
        wv[0], iv[0], precision=lax.Precision.HIGHEST, preferred_element_type=F32
    ).astype(BF16)
    gsend[...] = green.reshape(16, 40, 128)
    pl.semaphore_wait(pltpu.get_barrier_semaphore(), 34)

    def each_other(step):
        def run(d, _):
            step(d)
            return 0

        lax.fori_loop(1, 16, run, 0)

    def peer(d):
        return (a + d) % 16

    def green_copy(d):
        return remote(
            gsend.at[peer(d)], g1.at[a], a_send.at[d], a_recv.at[d], at(peer(d), y, z, c)
        )

    each_other(lambda d: green_copy(d).start())
    g1[a] = gsend[a]

    load(2).wait()

    def turn_half(i, _):
        n0 = pl.multiple_of(i * 16, 16)
        ht[:, pl.ds(n0, 16), :] = jnp.swapaxes(hv[pl.ds(n0, 16)], 0, 1)
        return 0

    lax.fori_loop(0, 12, turn_half, 0)

    load(3).wait()

    def turn_full(group, target):
        def turn(i, _):
            n0 = pl.multiple_of(i * 16, 16)
            target[:, pl.ds(n0, 16), :] = jnp.swapaxes(
                fv[pl.ds(n0, 16), group * 8 : group * 8 + 8, :], 0, 1
            )
            return 0

        lax.fori_loop(0, 12, turn, 0)

    def turn_given(i):
        for core in range(2):

            @pl.when(c == core)
            def _(core=core):
                turn_full(2 * (1 - core) + i, given.at[i])

    def turn_kept(i):
        for core in range(2):

            @pl.when(c == core)
            def _(core=core):
                turn_full(2 * core + i, ct.at[i, :, core])

    def give(i):
        source = ct.at[2, :, c] if i == 2 else given.at[i]
        return remote(source, ct.at[i, :, c], ct_send.at[i], ct_recv.at[i], sibling)

    turn_given(0)
    give(0).start()

    each_other(lambda d: green_copy(d).wait())

    def slot(yy, zz):
        return c * 8 + yy * 2 + zz

    own = slot(y, z)
    blocks[own] = jnp.swapaxes(g1[...], 0, 1)
    first, second = pl.ds(0, 20), pl.ds(20, 20)

    def spread(index):
        yy, zz, rows, target = (
            (y, z, None, to_up),
            (y, z, None, to_down),
            (y, z, None, to_z),
            (y, z, None, sibling),
            (y, 1 - z, None, to_up),
            (y, 1 - z, None, to_down),
            (y, 1 - z, None, sibling),
            (down, z, first, to_up),
            (down, z, None, sibling),
            (up, z, second, to_down),
            (up, z, None, sibling),
            (down, 1 - z, first, to_up),
            (down, 1 - z, None, sibling),
            (up, 1 - z, second, to_down),
            (up, 1 - z, None, sibling),
            (far, z, None, sibling),
            (far, 1 - z, None, sibling),
        )[index]
        ref = blocks.at[slot(yy, zz)]
        ref = ref if rows is None else ref.at[rows]
        return remote(ref, ref, g_send.at[index], g_recv.at[index], target)

    for index in (0, 1, 2, 3):
        spread(index).start()
    turn_given(1)
    give(1).start()

    @pl.when(c == 0)
    def _():
        turn_full(4, ct.at[2, :, 0])

    @pl.when(c == 1)
    def _():
        turn_full(4, ct.at[2, :, 1])

    spread(2).wait_recv()
    for index in (4, 5, 6):
        spread(index).start()
    spread(0).wait_recv()
    spread(1).wait_recv()
    for index in (7, 9, 8, 10):
        spread(index).start()
    give(2).start()
    turn_kept(0)
    spread(4).wait_recv()
    spread(5).wait_recv()
    for index in (11, 13, 12, 14):
        spread(index).start()
    turn_kept(1)
    load(4).wait()
    draws_by_slot = jnp.swapaxes(dv[...].T.reshape(16, 16, 192), 0, 1).reshape(8, 2, 16, 192)
    spread(7).wait_recv()
    spread(9).wait_recv()
    spread(15).start()
    spread(11).wait_recv()
    spread(13).wait_recv()
    spread(16).start()
    for index in (3, 6, 8, 10, 12, 14, 15, 16):
        spread(index).wait_recv()

    def bias_step(i, acc):
        p0 = i * 8
        left = jnp.concatenate([blocks[:, p0 + q].reshape(256, 128) for q in range(8)], axis=1)
        right = jnp.concatenate([ht[p0 + q] for q in range(8)], axis=1)
        return acc + lax.dot_general(
            left, right, (((1,), (1,)), ((), ())), preferred_element_type=F32
        )

    partial = lax.fori_loop(0, 5, bias_step, jnp.zeros((256, 192), F32))
    pb[...] = partial.astype(BF16).reshape(16, 16, 192)

    def part_copy(d):
        return remote(
            pb.at[peer(d)], parts_in.at[a], p_send.at[d], p_recv.at[d], at(peer(d), y, z, c)
        )

    each_other(lambda d: part_copy(d).start())
    parts_in[a] = pb[a]
    each_other(lambda d: part_copy(d).wait_recv())
    ball[a] = jnp.sum(parts_in[...].astype(F32), axis=0).astype(BF16)

    def bias_copy(d):
        return remote(ball.at[a], ball.at[a], b_send.at[d], b_recv.at[d], at(peer(d), y, z, c))

    def bias_from(d):
        there = ball.at[peer(16 - d)]
        return remote(there, there, b_send.at[d], b_recv.at[d], at(peer(16 - d), y, z, c))

    each_other(lambda d: bias_copy(d).start())
    each_other(lambda d: bias_from(d).wait_recv())
    bias = jnp.swapaxes(ball[...].astype(F32).reshape(2, 8, 16, 192), 0, 1)
    shifted = draws_by_slot - bias
    for owner in range(2):
        field[c, owner] = shifted[:, owner].astype(BF16)
    field_copy = remote(field.at[c], field.at[c], f_send, f_recv, sibling)
    field_copy.start()
    for i in range(3):
        give(i).wait_recv()
    field_copy.wait_recv()

    low, high = pl.ds(0, 4), pl.ds(4, 4)

    def owner_of(k):
        return c if k == 4 else k % 2

    def group_of(k):
        return 4 if k == 4 else 2 * c + k // 2

    def multiply(k):
        owner = owner_of(k)
        left = [field[s, owner].reshape(128, 192) for s in range(2)]

        def row(r, _):
            value = jnp.dot(left[0], ct[k // 2, r, 0], preferred_element_type=F32)
            value = value + jnp.dot(left[1], ct[k // 2, r, 1], preferred_element_type=F32)
            part[k, :, :, r] = value.astype(BF16).reshape(4, 2, 16, 640)
            return 0

        lax.fori_loop(0, 8, row, 0)

    def send_up(k, step):
        if k == 4:
            pair = (
                (zsum.at[far, low], z_pass_up),
                (zsum.at[up, high], z_from_down.at[high]),
                (z_pass_up, z_from_down.at[low]),
            )[step]
        else:
            pair = (
                (part.at[k, far, :, low], pass_up.at[k]),
                (part.at[k, up, :, high], from_down.at[k, :, high]),
                (pass_up.at[k], from_down.at[k, :, low]),
            )[step]
        return remote(pair[0], pair[1], s_up.at[k, step], r_up.at[k, step], to_up)

    def send_down(k, step):
        if k == 4:
            pair = (
                (zsum.at[far, high], z_pass_down),
                (zsum.at[down, low], z_from_up.at[low]),
                (z_pass_down, z_from_up.at[high]),
            )[step]
        else:
            pair = (
                (part.at[k, far, :, high], pass_down.at[k]),
                (part.at[k, down, :, low], from_up.at[k, :, low]),
                (pass_down.at[k], from_up.at[k, :, high]),
            )[step]
        return remote(pair[0], pair[1], s_down.at[k, step], r_down.at[k, step], to_down)

    def begin(k):
        for step in range(2):
            send_up(k, step).start()
            send_down(k, step).start()

    def pass_on(k):
        send_up(k, 0).wait_recv()
        if k == 4:
            z_pass_up[...] = (z_pass_up[...].astype(F32) + zsum[up, 0:4].astype(F32)).astype(BF16)
        else:
            pass_up[k] = (pass_up[k].astype(F32) + part[k, up, :, 0:4].astype(F32)).astype(BF16)
        send_up(k, 2).start()
        send_down(k, 0).wait_recv()
        if k == 4:
            z_pass_down[...] = (
                z_pass_down[...].astype(F32) + zsum[down, 4:8].astype(F32)
            ).astype(BF16)
        else:
            pass_down[k] = (
                pass_down[k].astype(F32) + part[k, down, :, 4:8].astype(F32)
            ).astype(BF16)
        send_down(k, 2).start()

    def gathered(k):
        for step in (1, 2):
            send_up(k, step).wait_recv()
            send_down(k, step).wait_recv()

    def z_copy(k):
        if k == 4:
            return remote(part.at[4, :, 1 - z], zin, z_send.at[4], z_recv.at[4], to_z)
        return remote(z_out.at[k], from_z.at[k], z_send.at[k], z_recv.at[k], to_z)

    def over_z(k):
        gathered(k)
        other = 1 - z
        total = part[k, y, other].astype(F32) + from_down[k, other].astype(F32)
        z_out[k] = (total + from_up[k, other].astype(F32)).astype(BF16)
        z_copy(k).start()

    def owner_copy(k, d):
        return remote(
            turned.at[k, peer(d)], operator.at[a, group_of(k)],
            o_send.at[k, d], o_recv.at[group_of(k), d], at(peer(d), y, z, owner_of(k)),
        )

    def deliver(k):
        if k == 4:
            gathered(4)
            total = zsum[y].astype(F32) + z_from_down[...].astype(F32)
            total = total + z_from_up[...].astype(F32)
        else:
            z_copy(k).wait_recv()
            total = part[k, y, z].astype(F32) + from_down[k, z].astype(F32)
            total = total + from_up[k, z].astype(F32) + from_z[k].astype(F32)
        turned[k] = jnp.swapaxes(total, 0, 1).astype(BF16)
        each_other(lambda d: owner_copy(k, d).start())
        if k == 4:
            operator[a, 4] = turned[k, a]
        else:

            @pl.when(c == k % 2)
            def _():
                operator[a, group_of(k)] = turned[k, a]

            @pl.when(c != k % 2)
            def _():
                owner_copy(k, 0).start()

    multiply(0)
    begin(0)
    multiply(4)
    z_copy(4).start()
    multiply(1)
    begin(1)
    aux_out[...] = jnp.swapaxes(shifted.reshape(16, 16, 192), 0, 1).reshape(256, 192).T
    multiply(2)
    pass_on(0)
    begin(2)
    multiply(3)
    pass_on(1)
    begin(3)
    over_z(0)
    z_copy(4).wait_recv()
    zsum[...] = (part[4, :, z].astype(F32) + zin[...].astype(F32)).astype(BF16)
    pass_on(2)
    deliver(0)
    over_z(1)
    pass_on(3)
    begin(4)
    deliver(1)
    over_z(2)
    over_z(3)
    pass_on(4)
    deliver(2)
    deliver(3)
    deliver(4)

    each_other(lambda d: part_copy(d).wait_send())
    each_other(lambda d: bias_copy(d).wait_send())
    for index in range(17):
        spread(index).wait_send()
    for i in range(3):
        give(i).wait_send()
    field_copy.wait_send()
    for k in range(5):
        for step in range(3):
            send_up(k, step).wait_send()
            send_down(k, step).wait_send()
        z_copy(k).wait_send()
        each_other(lambda d, k=k: owner_copy(k, d).wait_send())
        if k < 4:

            @pl.when(c != k % 2)
            def _(k=k):
                owner_copy(k, 0).wait_send()

    def arrival(group, d):
        return remote(
            turned.at[0, 0], operator.at[0, group], o_send.at[0, 0], o_recv.at[group, d], sibling
        )

    for group in range(5):
        each_other(lambda d, group=group: arrival(group, d).wait_recv())
        if group < 4:

            @pl.when(c != group // 2)
            def _(group=group):
                arrival(group, 0).wait_recv()

    matrix = operator[...].reshape(640, 640)
    term = wv[0]
    total = term
    for degree in range(1, 5):
        term = jnp.dot(matrix, term.astype(BF16), preferred_element_type=F32) * (1.0 / degree)
        total = total + term
    out[0] = total


def hand_over(walkers_in, aux_in, walkers_out, aux_out, walkers, aux, sem):
    ins = [
        pltpu.make_async_copy(walkers_in, walkers, sem.at[0]),
        pltpu.make_async_copy(aux_in, aux, sem.at[1]),
    ]
    outs = [
        pltpu.make_async_copy(walkers, walkers_out, sem.at[2]),
        pltpu.make_async_copy(aux, aux_out, sem.at[3]),
    ]
    for copy in ins:
        copy.start()
    for copy, following in zip(ins, outs):
        copy.wait()
        following.start()
    for copy in outs:
        copy.wait()


def shape(*dims, dtype=BF16):
    return jax.ShapeDtypeStruct(dims, dtype)


def room(*dims, dtype=BF16):
    return pltpu.VMEM(dims, dtype)


def dma(*dims):
    return pltpu.SemaphoreType.DMA(dims)


def body(walkers, intersection_inverse, aux_draws, chol_half, chol_full):
    new_walkers, aux = pl.pallas_call(
        kernel,
        out_shape=(shape(1, 640, 128, dtype=F32), shape(192, 256, dtype=F32)),
        in_specs=[ANY] * 5,
        out_specs=(VMEM, VMEM),
        scratch_shapes=[
            room(1, 640, 128, dtype=F32),
            room(1, 128, 128, dtype=F32),
            room(192, 256, dtype=F32),
            room(192, 40, 128),
            room(192, 40, 640),
            room(16, 40, 128),
            room(16, 40, 128),
            room(16, 40, 16, 128),
            room(40, 192, 128),
            room(3, 8, 2, 192, 640),
            room(2, 8, 192, 640),
            room(16, 16, 192),
            room(16, 16, 192),
            room(16, 16, 192),
            room(2, 2, 8, 16, 192),
            room(5, 4, 2, 8, 16, 640),
            room(4, 2, 4, 16, 640),
            room(4, 2, 4, 16, 640),
            room(4, 2, 8, 16, 640),
            room(4, 2, 8, 16, 640),
            room(4, 8, 16, 640),
            room(4, 8, 16, 640),
            room(4, 8, 16, 640),
            room(4, 8, 16, 640),
            room(4, 16, 640),
            room(4, 16, 640),
            room(8, 16, 640),
            room(8, 16, 640),
            room(5, 16, 8, 640),
            room(16, 5, 8, 640),
            dma(5), dma(3), dma(3), dma(16), dma(16), dma(17), dma(17), dma(16), dma(16), dma(16), dma(16),
            dma(), dma(), dma(5, 3), dma(5, 3), dma(5, 3), dma(5, 3), dma(5), dma(5), dma(5, 16), dma(5, 16),
        ],
        compiler_params=pltpu.CompilerParams(
            collective_id=0, has_side_effects=True, vmem_limit_bytes=60 * 2**20
        ),
        name="propagate",
    )(walkers, intersection_inverse, aux_draws.T, chol_half, chol_full)
    new_walkers, aux = pl.pallas_call(
        hand_over,
        out_shape=(shape(1, 640, 128, dtype=F32), shape(192, 256, dtype=F32)),
        in_specs=[ANY] * 2,
        out_specs=(ANY, ANY),
        scratch_shapes=[room(1, 640, 128, dtype=F32), room(192, 256, dtype=F32), dma(4)],
        name="hand_over",
    )(new_walkers, aux)
    return new_walkers, aux.T


def solution(mesh):
    placed = (
        P(("walk", "chol"), None, None),
        P(("walk", "chol"), None, None),
        P(None, "chol"),
        P("chol", "walk", None),
        P("chol", "walk", None),
    )
    return jax.shard_map(
        body,
        mesh=mesh,
        in_specs=placed,
        out_specs=(P(("walk", "chol"), None, None), P(None, "chol")),
        check_vma=False,
    )
```

```python
import jax
import jax.numpy as jnp
from jax import lax
from jax.experimental import pallas as pl
from jax.experimental.pallas import tpu as pltpu
from jax.sharding import PartitionSpec as P

MESH = pl.DeviceIdType.MESH
BF16 = jnp.bfloat16
F32 = jnp.float32
ANY = pl.BlockSpec(memory_space=pl.ANY)
VMEM = pl.BlockSpec(memory_space=pltpu.VMEM)


def place():
    a = lax.axis_index("walk")
    b = lax.axis_index("chol")
    return a, b // 4, (b // 2) % 2, b % 2


def at(a, y, z, c):
    return (a, y * 4 + z * 2 + c)


def remote(src, dst, send, recv, target):
    return pltpu.make_async_remote_copy(
        src_ref=src, dst_ref=dst, send_sem=send, recv_sem=recv, device_id=target, device_id_type=MESH
    )


def settle(ref, sem):
    a, y, z, c = place()
    remote(ref, ref, sem, sem, at(a, y, z, 1 - c)).wait_recv()


def greet(target):
    pl.semaphore_signal(pltpu.get_barrier_semaphore(), inc=1, device_id=target, device_id_type=MESH)


def kernel(
    walkers, inverse, draws, half, full,
    out, aux_out,
    wv, iv, dv, hv, fv, gsend, blocks, gt, ht, ct, given, dj, pb, xin, zhin, ball, field,
    part, pass_up, pass_down, from_down, from_up, z_out, from_z,
    zin, zsum, z_pass_up, z_pass_down, z_from_down, z_from_up, turned, operator, term1,
    in_sem, ct_send, ct_recv, a_send, a_recv, g_send, g_recv, p_send, p_recv, q_send, q_recv,
    b_send, b_recv, f_send, f_recv, y_send, far_in, near_in, last_in, z_send, z_in, o_send, o_recv,
):
    a, y, z, c = place()
    x, zh = a // 4, a % 4
    up, down, far = (y + 1) % 4, (y + 3) % 4, (y + 2) % 4
    to_up, to_down, to_z = at(a, up, z, c), at(a, down, z, c), at(a, y, 1 - z, c)
    sibling = at(a, y, z, 1 - c)

    def load(index):
        pair = ((walkers, wv), (inverse, iv), (half, hv), (full, fv), (draws, dv))[index]
        return pltpu.make_async_copy(pair[0], pair[1], in_sem.at[index])

    for index in range(5):
        load(index).start()

    def greet_walk(d, _):
        greet(at((a + d) % 16, y, z, c))
        greet(at((a + d) % 16, y, z, 1 - c))
        return 0

    lax.fori_loop(1, 16, greet_walk, 0)
    round_chol = (
        at(a, far, 1 - z, c), at(a, far, z, c), at(a, up, 1 - z, c), at(a, down, 1 - z, c),
        to_up, to_down, to_z, sibling,
    )
    for target in round_chol:
        greet(target)

    load(0).wait()
    load(1).wait()
    green = jnp.dot(
        wv[0], iv[0], precision=lax.Precision.HIGHEST, preferred_element_type=F32
    ).astype(BF16)
    gsend[...] = green.reshape(16, 40, 128)
    pl.semaphore_wait(pltpu.get_barrier_semaphore(), 38)

    def each_other(step):
        def run(d, _):
            step(d)
            return 0

        lax.fori_loop(1, 16, run, 0)

    def peer(d):
        return (a + d) % 16

    def slot(yy, zz):
        return c * 8 + yy * 2 + zz

    own = slot(y, z)

    def green_copy(to):
        return remote(
            gsend.at[to], blocks.at[own, a % 2, a // 2], a_send, a_recv.at[a % 2], at(to, y, z, c)
        )

    each_other(lambda d: green_copy(peer(d)).start())
    blocks[own, a % 2, a // 2] = gsend[a]

    load(2).wait()

    def turn_half(i, _):
        n0 = pl.multiple_of(i * 16, 16)
        ht[:, pl.ds(n0, 16), :] = jnp.swapaxes(hv[pl.ds(n0, 16)], 0, 1)
        return 0

    lax.fori_loop(0, 12, turn_half, 0)

    load(3).wait()

    def turn_full(group, target):
        def turn(i, _):
            n0 = pl.multiple_of(i * 16, 16)
            target[:, pl.ds(n0, 16), :] = jnp.swapaxes(
                fv[pl.ds(n0, 16), group * 8 : group * 8 + 8, :], 0, 1
            )
            return 0

        lax.fori_loop(0, 12, turn, 0)

    def turn_given(i):
        for core in range(2):

            @pl.when(c == core)
            def _(core=core):
                turn_full(2 * (1 - core) + i, given.at[i])

    def turn_kept(i):
        for core in range(2):

            @pl.when(c == core)
            def _(core=core):
                turn_full(2 * core + i, ct.at[i, :, core])

    def give(i):
        source = ct.at[2, :, c] if i == 2 else given.at[i]
        return remote(source, ct.at[i, :, c], ct_send, ct_recv, sibling)

    turn_given(0)
    give(0).start()

    def wait_green(h):
        @pl.when(a % 2 == h)
        def _():
            settle(blocks.at[0, h, pl.ds(0, 7)], a_recv.at[h])

        @pl.when(a % 2 != h)
        def _():
            settle(blocks.at[0, h], a_recv.at[h])

    origins = (
        (far, 1 - z), (far, z), (down, 1 - z), (up, 1 - z), (down, z), (up, z), (y, 1 - z),
    )

    def spread(h, index):
        yy, zz = (y, z) if index < 8 else origins[index - 8]
        target = round_chol[index] if index < 8 else sibling
        ref = blocks.at[slot(yy, zz), h]
        return remote(ref, ref, g_send, g_recv.at[h, min(index, 7)], target)

    def spread_own(h):
        for index in range(8):
            spread(h, index).start()

    def spread_on(h):
        for index in (6, 5, 4, 3, 2, 1, 0):
            settle(blocks.at[0, h], g_recv.at[h, index])
            spread(h, 8 + index).start()
        settle(blocks.at[pl.ds(0, 4)], g_recv.at[h, 7])

    def bias_sums(h):
        def turn(i, _):
            both = blocks[pl.ds(2 * i, 2), h].reshape(16, 40, 128)
            gt[h, :, i] = jnp.swapaxes(both, 0, 1)
            return 0

        lax.fori_loop(0, 8, turn, 0)

        def step(i, acc):
            p0 = i * 8
            left = jnp.concatenate([gt[h, p0 + q].reshape(128, 128) for q in range(8)], axis=1)
            right = jnp.concatenate([ht[p0 + q] for q in range(8)], axis=1)
            return acc + lax.dot_general(
                left, right, (((1,), (1,)), ((), ())), preferred_element_type=F32
            )

        partial = lax.fori_loop(0, 5, step, jnp.zeros((128, 192), F32))
        pb[4 * h : 4 * h + 4] = partial.astype(BF16).reshape(4, 32, 192)

    def x_peer(e):
        return (x + e) % 4

    def x_copy(h, e):
        return remote(
            pb.at[4 * h + x_peer(e)], xin.at[h, x], p_send, p_recv.at[h],
            at(x_peer(e) * 4 + zh, y, z, c),
        )

    def zh_copy(h, e):
        ref = zhin.at[h, zh]
        return remote(ref, ref, q_send, q_recv.at[h], at(x * 4 + (zh + e) % 4, y, z, c))

    def back_copy(h, e):
        ref = ball.at[h, x]
        return remote(ref, ref, b_send, b_recv.at[h], at(x_peer(e) * 4 + zh, y, z, c))

    def start_x(h):
        for e in (2, 1, 3):
            x_copy(h, e).start()
        xin[h, x] = pb[4 * h + x]

    def start_zh(h):
        settle(xin.at[h, pl.ds(0, 3)], p_recv.at[h])
        zhin[h, zh] = jnp.sum(xin[h].astype(F32), axis=0).astype(BF16)
        for e in (2, 1, 3):
            zh_copy(h, e).start()

    def start_back(h):
        settle(zhin.at[h, pl.ds(0, 3)], q_recv.at[h])
        ball[h, x] = jnp.sum(zhin[h].astype(F32), axis=0).astype(BF16)
        for e in (2, 1, 3):
            back_copy(h, e).start()

    def field_copy(h):
        ref = field.at[c, h]
        return remote(ref, ref, f_send, f_recv.at[h], sibling)

    def field_arrived(h):
        settle(field.at[0, h], f_recv.at[h])

    def shift(h):
        settle(ball.at[h, pl.ds(0, 3)], b_recv.at[h])
        shifted = dj[h] - ball[h].astype(F32).reshape(2, 8, 8, 192)
        dj[h] = shifted
        field[c, h] = shifted.astype(BF16).reshape(2, 64, 192)
        field_copy(h).start()

    wait_green(0)
    spread_own(0)
    wait_green(1)
    spread_own(1)
    turn_given(1)
    give(1).start()
    for core in range(2):

        @pl.when(c == core)
        def _(core=core):
            turn_full(4, ct.at[2, :, core])

    give(2).start()
    turn_kept(0)
    turn_kept(1)
    load(4).wait()
    by_walker = dv[...].T.reshape(8, 2, 16, 192)
    for h in range(2):
        half_draws = jnp.swapaxes(by_walker[:, h], 0, 1).reshape(8, 2, 8, 192)
        for core in range(2):
            dj[h, core] = half_draws[:, core]
    spread_on(0)
    bias_sums(0)
    start_x(0)
    start_zh(0)
    spread_on(1)
    bias_sums(1)
    start_x(1)
    start_back(0)
    start_zh(1)
    shift(0)
    settle(ct.at[:, :, 1 - c], ct_recv)
    field_arrived(0)

    low, high = pl.ds(0, 4), pl.ds(4, 4)

    def multiply(pair, first_row, last_row):
        left = [field[s, pair // 2].reshape(128, 192) for s in range(2)]

        def row(r, _):
            value = jnp.dot(left[0], ct[pair % 2, r, 0], preferred_element_type=F32)
            value = value + jnp.dot(left[1], ct[pair % 2, r, 1], preferred_element_type=F32)
            value = value.astype(BF16).reshape(2, 4, 2, 8, 640)
            for core in range(2):
                part[2 * pair + core, :, :, r] = value[core]
            return 0

        lax.fori_loop(first_row, last_row, row, 0)

    def multiply_z(h):
        left = [field[s, h, c] for s in range(2)]

        def row(r, _):
            value = jnp.dot(left[0], ct[2, r, 0], preferred_element_type=F32)
            value = value + jnp.dot(left[1], ct[2, r, 1], preferred_element_type=F32)
            part[8 + h, :, :, r] = value.astype(BF16).reshape(4, 2, 8, 640)
            return 0

        lax.fori_loop(0, 8, row, 0)
        z_copy(8 + h).start()

    def z_copy(k):
        if k >= 8:
            return remote(part.at[k, :, 1 - z], zin.at[k - 8], z_send, z_in.at[k - 8], to_z)
        return remote(z_out.at[k], from_z.at[k], z_send, last_in.at[k], to_z)

    def sum_z(k):
        settle(zin.at[k - 8], z_in.at[k - 8])
        total = part[k, :, z].astype(F32) + zin[k - 8].astype(F32)
        zsum[k - 8] = total.astype(BF16)

    def arrivals(k, step):
        return (far_in, near_in, near_in, last_in)[step].at[k]

    def send_up(k, step):
        if k >= 8:
            pair = (
                (zsum.at[k - 8, far, low], z_pass_up.at[k - 8]),
                (zsum.at[k - 8, up, high], z_from_down.at[k - 8, high]),
                (z_pass_up.at[k - 8], z_from_down.at[k - 8, low]),
            )[step]
        else:
            pair = (
                (part.at[k, far, :, low], pass_up.at[k]),
                (part.at[k, up, :, high], from_down.at[k, :, high]),
                (pass_up.at[k, 1 - z], from_down.at[k, 1 - z, low]),
                (pass_up.at[k, z], from_down.at[k, z, low]),
            )[step]
        return remote(pair[0], pair[1], y_send.at[k // 8], arrivals(k, step), to_up)

    def send_down(k, step):
        if k >= 8:
            pair = (
                (zsum.at[k - 8, far, high], z_pass_down.at[k - 8]),
                (zsum.at[k - 8, down, low], z_from_up.at[k - 8, low]),
                (z_pass_down.at[k - 8], z_from_up.at[k - 8, high]),
            )[step]
        else:
            pair = (
                (part.at[k, far, :, high], pass_down.at[k]),
                (part.at[k, down, :, low], from_up.at[k, :, low]),
                (pass_down.at[k, 1 - z], from_up.at[k, 1 - z, high]),
                (pass_down.at[k, z], from_up.at[k, z, high]),
            )[step]
        return remote(pair[0], pair[1], y_send.at[k // 8], arrivals(k, step), to_down)

    def begin(k, *which):
        for step in which or (0, 1):
            send_up(k, step).start()
            send_down(k, step).start()

    def pass_on(k):
        settle(z_from_down.at[k - 8] if k >= 8 else from_down.at[k], far_in.at[k])
        if k >= 8:
            total = z_pass_up[k - 8].astype(F32) + zsum[k - 8, up, 0:4].astype(F32)
            z_pass_up[k - 8] = total.astype(BF16)
            send_up(k, 2).start()
            total = z_pass_down[k - 8].astype(F32) + zsum[k - 8, down, 4:8].astype(F32)
            z_pass_down[k - 8] = total.astype(BF16)
            send_down(k, 2).start()
            return
        for zz, step in ((1 - z, 2), (z, 3)):
            total = pass_up[k, zz].astype(F32) + part[k, up, zz, 0:4].astype(F32)
            pass_up[k, zz] = total.astype(BF16)
            send_up(k, step).start()
            total = pass_down[k, zz].astype(F32) + part[k, down, zz, 4:8].astype(F32)
            pass_down[k, zz] = total.astype(BF16)
            send_down(k, step).start()

    def gathered(k):
        settle(from_down.at[0] if k >= 8 else pass_up.at[pl.ds(0, 3)], near_in.at[k])

    def over_z(k):
        gathered(k)
        other = 1 - z
        total = part[k, y, other].astype(F32) + from_down[k, other].astype(F32)
        z_out[k] = (total + from_up[k, other].astype(F32)).astype(BF16)
        z_copy(k).start()

    def group_of(k):
        return 4 if k >= 8 else 2 * c + (k // 2) % 2

    def core_of(k):
        return c if k >= 8 else k % 2

    def half_of(k):
        return k - 8 if k >= 8 else k // 4

    def walk_of(k, i):
        return 2 * i + half_of(k)

    def owner_copy(k, i):
        group = group_of(k)
        return remote(
            turned.at[8 * k + i], operator.at[group, a], o_send, o_recv.at[group],
            at(walk_of(k, i), y, z, core_of(k)),
        )

    def each_owner(k, other, own=None):
        def run(d, _):
            i = (a + d) % 8
            here = jnp.logical_and(walk_of(k, i) == a, core_of(k) == c)

            @pl.when(jnp.logical_not(here))
            def _():
                other(i)

            if own is not None:

                @pl.when(here)
                def _():
                    own(i)

            return 0

        lax.fori_loop(0, 8, run, 0)

    def deliver(k):
        if k >= 8:
            gathered(k)
            total = zsum[k - 8, y].astype(F32) + z_from_down[k - 8].astype(F32)
            total = total + z_from_up[k - 8].astype(F32)
        else:
            settle(from_down.at[k], last_in.at[k])
            total = part[k, y, z].astype(F32) + from_down[k, z].astype(F32)
            total = total + from_up[k, z].astype(F32) + from_z[k].astype(F32)
        turned[8 * k : 8 * k + 8] = jnp.swapaxes(total, 0, 1).astype(BF16)

        def keep(i):
            operator[group_of(k), a] = turned[8 * k + i]

        each_owner(k, lambda i: owner_copy(k, i).start(), keep)

    multiply(0, 0, 4)
    send_up(0, 0).start()
    send_down(0, 1).start()
    multiply(0, 4, 8)
    send_down(0, 0).start()
    send_up(0, 1).start()
    begin(1)
    multiply_z(0)
    multiply(1, 0, 8)
    start_back(1)
    pass_on(0)
    begin(2)
    pass_on(1)
    begin(3)
    shift(1)
    field_arrived(1)
    multiply_z(1)
    multiply(2, 0, 8)
    over_z(0)
    pass_on(2)
    begin(4)
    multiply(3, 0, 8)
    over_z(1)
    pass_on(3)
    begin(5)
    sum_z(8)
    begin(8)
    by_half = [
        jnp.swapaxes(jnp.swapaxes(dj[h], 0, 1).reshape(16, 8, 192), 0, 1) for h in range(2)
    ]
    aux_out[...] = jnp.stack(by_half, axis=1).reshape(256, 192).T
    over_z(2)
    pass_on(4)
    begin(6)
    deliver(0)
    deliver(1)
    over_z(3)
    pass_on(5)
    deliver(2)
    pass_on(8)
    begin(7)
    deliver(3)
    over_z(4)
    pass_on(6)
    sum_z(9)
    begin(9, 0)
    deliver(4)
    over_z(5)
    deliver(8)
    pass_on(7)
    begin(9, 1)
    deliver(5)
    over_z(6)
    pass_on(9)
    over_z(7)
    deliver(6)
    deliver(9)
    deliver(7)

    settle(gsend.at[pl.ds(0, 15)], a_send)
    settle(ct.at[:, :, c], ct_send)
    settle(blocks.at[pl.ds(0, 15)], g_send)
    settle(pb.at[pl.ds(0, 6)], p_send)
    settle(pb.at[pl.ds(0, 6)], q_send)
    settle(pb.at[pl.ds(0, 6)], b_send)
    settle(field.at[0], f_send)
    settle(part.at[pl.ds(0, 6)], y_send.at[0])
    settle(pass_up.at[pl.ds(0, 6)], y_send.at[1])
    settle(from_down, z_send)

    def wait_group(group):
        core = c if group == 4 else group // 2

        @pl.when(core == c)
        def _():
            settle(operator.at[group, pl.ds(0, 15)], o_recv.at[group])

        @pl.when(core != c)
        def _():
            settle(operator.at[group], o_recv.at[group])

    start_low = wv[0].astype(BF16)
    for group in (0, 2, 1, 3, 4):
        wait_group(group)
        rows = operator[group].reshape(128, 640)
        value = jnp.dot(rows, start_low, preferred_element_type=F32)
        term1[:, group] = value.reshape(16, 8, 128)
    settle(turned.at[pl.ds(0, 77)], o_send)
    matrix = jnp.swapaxes(operator[...], 0, 1).reshape(640, 640)
    term = term1[...].reshape(640, 128)
    total = wv[0] + term
    for degree in range(2, 5):
        term = jnp.dot(matrix, term.astype(BF16), preferred_element_type=F32) * (1.0 / degree)
        total = total + term
    out[0] = total


def hand_over(walkers_in, aux_in, walkers_out, aux_out, walkers, aux, sem):
    ins = [
        pltpu.make_async_copy(walkers_in, walkers, sem.at[0]),
        pltpu.make_async_copy(aux_in, aux, sem.at[1]),
    ]
    outs = [
        pltpu.make_async_copy(walkers, walkers_out, sem.at[2]),
        pltpu.make_async_copy(aux, aux_out, sem.at[3]),
    ]
    for copy in ins:
        copy.start()
    for copy, following in zip(ins, outs):
        copy.wait()
        following.start()
    for copy in outs:
        copy.wait()


def shape(*dims, dtype=BF16):
    return jax.ShapeDtypeStruct(dims, dtype)


def room(*dims, dtype=BF16):
    return pltpu.VMEM(dims, dtype)


def dma(*dims):
    return pltpu.SemaphoreType.DMA(dims)


def body(walkers, intersection_inverse, aux_draws, chol_half, chol_full):
    new_walkers, aux = pl.pallas_call(
        kernel,
        out_shape=(shape(1, 640, 128, dtype=F32), shape(192, 256, dtype=F32)),
        in_specs=[ANY] * 5,
        out_specs=(VMEM, VMEM),
        scratch_shapes=[
            room(1, 640, 128, dtype=F32),
            room(1, 128, 128, dtype=F32),
            room(192, 256, dtype=F32),
            room(192, 40, 128),
            room(192, 40, 640),
            room(16, 40, 128),
            room(16, 2, 8, 40, 128),
            room(2, 40, 8, 16, 128),
            room(40, 192, 128),
            room(3, 8, 2, 192, 640),
            room(2, 8, 192, 640),
            room(2, 2, 8, 8, 192, dtype=F32),
            room(8, 32, 192),
            room(2, 4, 32, 192),
            room(2, 4, 32, 192),
            room(2, 4, 32, 192),
            room(2, 2, 2, 64, 192),
            room(10, 4, 2, 8, 8, 640),
            room(8, 2, 4, 8, 640),
            room(8, 2, 4, 8, 640),
            room(8, 2, 8, 8, 640),
            room(8, 2, 8, 8, 640),
            room(8, 8, 8, 640),
            room(8, 8, 8, 640),
            room(2, 4, 8, 8, 640),
            room(2, 4, 8, 8, 640),
            room(2, 4, 8, 640),
            room(2, 4, 8, 640),
            room(2, 8, 8, 640),
            room(2, 8, 8, 640),
            room(80, 8, 640),
            room(5, 16, 8, 640),
            room(16, 5, 8, 128, dtype=F32),
            dma(5), dma(), dma(), dma(), dma(2), dma(), dma(2, 8), dma(), dma(2), dma(), dma(2),
            dma(), dma(2), dma(), dma(2), dma(2), dma(10), dma(10), dma(8), dma(), dma(2), dma(), dma(5),
        ],
        compiler_params=pltpu.CompilerParams(
            collective_id=0, has_side_effects=True, vmem_limit_bytes=60 * 2**20
        ),
        name="propagate",
    )(walkers, intersection_inverse, aux_draws.T, chol_half, chol_full)
    new_walkers, aux = pl.pallas_call(
        hand_over,
        out_shape=(shape(1, 640, 128, dtype=F32), shape(192, 256, dtype=F32)),
        in_specs=[ANY] * 2,
        out_specs=(ANY, ANY),
        scratch_shapes=[room(1, 640, 128, dtype=F32), room(192, 256, dtype=F32), dma(4)],
        name="hand_over",
    )(new_walkers, aux)
    return new_walkers, aux.T


def solution(mesh):
    placed = (
        P(("walk", "chol"), None, None),
        P(("walk", "chol"), None, None),
        P(None, "chol"),
        P("chol", "walk", None),
        P("chol", "walk", None),
    )
    return jax.shard_map(
        body,
        mesh=mesh,
        in_specs=placed,
        out_specs=(P(("walk", "chol"), None, None), P(None, "chol")),
        check_vma=False,
    )
```

```python
import jax
import jax.numpy as jnp
from jax import lax
from jax.experimental import pallas as pl
from jax.experimental.pallas import tpu as pltpu
from jax.sharding import PartitionSpec as P

MESH = pl.DeviceIdType.MESH
BF16 = jnp.bfloat16
F32 = jnp.float32
ANY = pl.BlockSpec(memory_space=pl.ANY)
VMEM = pl.BlockSpec(memory_space=pltpu.VMEM)


def place():
    a = lax.axis_index("walk")
    b = lax.axis_index("chol")
    return a, b // 4, (b // 2) % 2, b % 2


def at(a, y, z, c):
    return (a, y * 4 + z * 2 + c)


def remote(src, dst, send, recv, target):
    return pltpu.make_async_remote_copy(
        src_ref=src, dst_ref=dst, send_sem=send, recv_sem=recv, device_id=target, device_id_type=MESH
    )


def settle(ref, sem):
    a, y, z, c = place()
    remote(ref, ref, sem, sem, at(a, y, z, 1 - c)).wait_recv()


def greet(target):
    pl.semaphore_signal(pltpu.get_barrier_semaphore(), inc=1, device_id=target, device_id_type=MESH)


def kernel(
    walkers, inverse, draws, half, full,
    out, aux_out,
    wv, iv, dv, hv, fv, gsend, blocks, gt, ht, ct, given, order, dj, pb, xin, zhin, ball, field,
    part, pass_up, pass_down, from_down, from_up, z_out, from_z,
    zin, zsum, z_pass_up, z_pass_down, z_from_down, z_from_up, turned, operator, term1,
    in_sem, ct_send, ct_recv, a_send, a_recv, g_send, g_recv, p_send, p_recv, q_send, q_recv,
    b_send, b_recv, f_send, f_recv, y_send, far_in, near_in, last_in, z_send, z_in, o_send, o_recv,
):
    a, y, z, c = place()
    x, zh = a // 4, a % 4
    up, down, far = (y + 1) % 4, (y + 3) % 4, (y + 2) % 4
    to_up, to_down, to_z = at(a, up, z, c), at(a, down, z, c), at(a, y, 1 - z, c)
    sibling = at(a, y, z, 1 - c)

    def load(index):
        pair = ((walkers, wv), (inverse, iv), (half, hv), (full, fv), (draws, dv))[index]
        return pltpu.make_async_copy(pair[0], pair[1], in_sem.at[index])

    for index in range(5):
        load(index).start()

    def greet_walk(d, _):
        greet(at((a + d) % 16, y, z, c))
        return 0

    lax.fori_loop(1, 16, greet_walk, 0)

    def greet_senders(d, _):
        xx, core = d // 2, d % 2

        @pl.when(jnp.logical_or(xx != x, core != c))
        def _():
            greet(at(xx * 4 + zh, y, z, core))

        greet(at(xx * 4 + (zh + 2) % 4, y, 1 - z, core))
        greet(at(xx * 4 + (zh + 3) % 4, y, 1, core))
        greet(at(xx * 4 + (zh + 1) % 4, y, 0, core))
        return 0

    lax.fori_loop(0, 8, greet_senders, 0)
    to_far = at(a, far, z, c)
    for target in (to_far, to_up, to_down, to_z, sibling):
        greet(target)

    load(0).wait()
    load(1).wait()
    green = jnp.dot(
        wv[0], iv[0], precision=lax.Precision.HIGHEST, preferred_element_type=F32
    ).astype(BF16)
    gsend[...] = green.reshape(16, 40, 128)
    pl.semaphore_wait(pltpu.get_barrier_semaphore(), 51)

    def each_other(step):
        def run(d, _):
            step(d)
            return 0

        lax.fori_loop(1, 16, run, 0)

    def peer(d):
        return (a + d) % 16

    def slot(yy, zz):
        return c * 8 + yy * 2 + zz

    own = slot(y, z)

    def green_copy(to):
        return remote(
            gsend.at[to], blocks.at[own, a % 2, a // 2], a_send, a_recv.at[a % 2], at(to, y, z, c)
        )

    @pl.when(a % 2 == 0)
    def _():
        each_other(lambda d: green_copy(peer(d)).start())

    blocks[own, a % 2, a // 2] = gsend[a]

    load(2).wait()

    def turn_half(i, _):
        n0 = pl.multiple_of(i * 16, 16)
        ht[:, pl.ds(n0, 16), :] = jnp.swapaxes(hv[pl.ds(n0, 16)], 0, 1)
        return 0

    lax.fori_loop(0, 12, turn_half, 0)

    load(3).wait()

    def turn_full(group, target):
        def turn(i, _):
            n0 = pl.multiple_of(i * 16, 16)
            target[:, pl.ds(n0, 16), :] = jnp.swapaxes(
                fv[pl.ds(n0, 16), group * 8 : group * 8 + 8, :], 0, 1
            )
            return 0

        lax.fori_loop(0, 12, turn, 0)

    def turn_given(i):
        for core in range(2):

            @pl.when(c == core)
            def _(core=core):
                turn_full(2 * (1 - core) + i, given.at[i])

    def turn_kept(i):
        for core in range(2):

            @pl.when(c == core)
            def _(core=core):
                turn_full(2 * core + i, ct.at[i, :, core])

    def give(i):
        source = ct.at[2, :, c] if i == 2 else given.at[i]
        return remote(source, ct.at[i, :, c], ct_send, ct_recv, sibling)

    turn_given(0)
    give(0).start()
    turn_given(1)
    give(1).start()
    for core in range(2):

        @pl.when(c == core)
        def _(core=core):
            turn_full(4, ct.at[2, :, core])

    give(2).start()

    @pl.when(a % 2 == 1)
    def _():
        each_other(lambda d: green_copy(peer(d)).start())

    turn_kept(0)
    turn_kept(1)

    def owner(h, zl, i):
        same = 1 - (zh + h) % 2
        pick = i % 2
        to_zh = (zh + same * 2 * pick + (1 - same) * (3 - 2 * zl)) % 4
        return i // 2, to_zh, same * ((zl + pick) % 2) + (1 - same) * pick

    for h in range(2):
        row = lax.broadcasted_iota(jnp.int32, (64, 64), 0)
        column = lax.broadcasted_iota(jnp.int32, (64, 64), 1)
        to_x, to_zh, to_zl = owner(h, (row // 8) % 2, row % 8)
        source = (row // 16) * 16 + to_zl * 8 + to_x * 2 + to_zh // 2
        order[h] = jnp.where(source == column, 1.0, 0.0).astype(BF16)

    load(4).wait()
    by_walker = dv[...].T.reshape(8, 2, 16, 192)
    for h in range(2):
        half_draws = jnp.swapaxes(by_walker[:, h], 0, 1).reshape(8, 2, 8, 192)
        for core in range(2):
            dj[h, core] = half_draws[:, core]

    def wait_green(h):
        @pl.when(a % 2 == h)
        def _():
            settle(blocks.at[0, h, pl.ds(0, 7)], a_recv.at[h])

        @pl.when(a % 2 != h)
        def _():
            settle(blocks.at[0, h], a_recv.at[h])

    def spread(h, index):
        yy, zz, target = (
            (y, z, to_far), (y, z, to_up), (y, z, to_down), (y, z, to_z), (y, z, sibling),
            (y, 1 - z, to_up), (y, 1 - z, to_down), (far, z, to_z),
            (y, 1 - z, sibling), (far, z, sibling), (down, z, sibling), (up, z, sibling),
            (down, 1 - z, sibling), (up, 1 - z, sibling), (far, 1 - z, sibling),
        )[index]
        ref = blocks.at[slot(yy, zz), h]
        return remote(ref, ref, g_send, g_recv.at[h, index if index < 8 else 4], target)

    def start(h, *indices):
        for index in indices:
            spread(h, index).start()

    def landed(h, index):
        settle(blocks.at[0, h], g_recv.at[h, index])

    def spread_own(h):
        start(h, 3, 0, 1, 2, 4)

    def spread_second(h):
        landed(h, 3)
        start(h, 5, 6, 8)
        landed(h, 0)
        start(h, 7, 9)

    def spread_on(h):
        for index in (1, 2, 5, 6, 7):
            landed(h, index)
            start(h, {1: 10, 2: 11, 5: 12, 6: 13, 7: 14}[index])
        settle(blocks.at[pl.ds(0, 4)], g_recv.at[h, 4])

    def bias_sums(h):
        def turn(i, _):
            both = blocks[pl.ds(2 * i, 2), h].reshape(16, 40, 128)
            gt[h, :, i] = jnp.swapaxes(both, 0, 1)
            return 0

        lax.fori_loop(0, 8, turn, 0)

        def step(i, acc):
            p0 = i * 8
            left = jnp.concatenate([gt[h, p0 + q].reshape(128, 128) for q in range(8)], axis=1)
            right = jnp.concatenate([ht[p0 + q] for q in range(8)], axis=1)
            return acc + lax.dot_general(
                left, right, (((1,), (1,)), ((), ())), preferred_element_type=F32
            )

        partial = lax.fori_loop(0, 5, step, jnp.zeros((128, 192), F32))
        pb[4 * h : 4 * h + 4] = partial.astype(BF16).reshape(4, 32, 192)

    def x_peer(e):
        return (x + e) % 4

    def x_copy(h, e):
        return remote(
            pb.at[4 * h + x_peer(e)], xin.at[h, x], p_send, p_recv.at[h],
            at(x_peer(e) * 4 + zh, y, z, c),
        )

    def zh_copy(h, e):
        ref = zhin.at[h, zh]
        return remote(ref, ref, q_send, q_recv.at[h], at(x * 4 + (zh + e) % 4, y, z, c))

    def back_copy(h, e):
        ref = ball.at[h, x]
        return remote(ref, ref, b_send, b_recv.at[h], at(x_peer(e) * 4 + zh, y, z, c))

    def start_x(h):
        for e in (2, 1, 3):
            x_copy(h, e).start()
        xin[h, x] = pb[4 * h + x]

    def start_zh(h):
        settle(xin.at[h, pl.ds(0, 3)], p_recv.at[h])
        zhin[h, zh] = jnp.sum(xin[h].astype(F32), axis=0).astype(BF16)
        for e in (2, 1, 3):
            zh_copy(h, e).start()

    def start_back(h):
        settle(zhin.at[h, pl.ds(0, 3)], q_recv.at[h])
        ball[h, x] = jnp.sum(zhin[h].astype(F32), axis=0).astype(BF16)
        for e in (2, 1, 3):
            back_copy(h, e).start()

    def field_copy(h):
        ref = field.at[c, h]
        return remote(ref, ref, f_send, f_recv.at[h], sibling)

    def field_arrived(h):
        settle(field.at[0, h], f_recv.at[h])

    def shift(h):
        settle(ball.at[h, pl.ds(0, 3)], b_recv.at[h])
        shifted = dj[h] - ball[h].astype(F32).reshape(2, 8, 8, 192)
        dj[h] = shifted
        for core in range(2):
            rows = shifted[core].astype(BF16).reshape(64, 192)
            rows = jnp.dot(order[h], rows, preferred_element_type=F32)
            field[c, h, core] = rows.astype(BF16)
        field_copy(h).start()

    wait_green(0)
    spread_own(0)
    spread_second(0)
    wait_green(1)
    spread_own(1)
    spread_on(0)
    bias_sums(0)
    start_x(0)
    spread_second(1)
    start_zh(0)
    spread_on(1)
    start_back(0)
    bias_sums(1)
    start_x(1)
    shift(0)
    settle(ct.at[:, :, 1 - c], ct_recv)
    field_arrived(0)

    low, high = pl.ds(0, 4), pl.ds(4, 4)

    def multiply(pair, first_row, last_row):
        left = [field[s, pair // 2].reshape(128, 192) for s in range(2)]

        def row(r, _):
            value = jnp.dot(left[0], ct[pair % 2, r, 0], preferred_element_type=F32)
            value = value + jnp.dot(left[1], ct[pair % 2, r, 1], preferred_element_type=F32)
            value = value.astype(BF16).reshape(2, 4, 2, 8, 640)
            for core in range(2):
                part[2 * pair + core, :, :, r] = value[core]
            return 0

        lax.fori_loop(first_row, last_row, row, 0)

    def multiply_z(h):
        left = [field[s, h, c] for s in range(2)]

        def row(r, _):
            value = jnp.dot(left[0], ct[2, r, 0], preferred_element_type=F32)
            value = value + jnp.dot(left[1], ct[2, r, 1], preferred_element_type=F32)
            part[8 + h, :, :, r] = value.astype(BF16).reshape(4, 2, 8, 640)
            return 0

        lax.fori_loop(0, 8, row, 0)
        z_copy(8 + h).start()

    def z_copy(k):
        if k >= 8:
            return remote(part.at[k, :, 1 - z], zin.at[k - 8], z_send, z_in.at[k - 8], to_z)
        return remote(z_out.at[k], from_z.at[k], z_send, last_in.at[k], to_z)

    def sum_z(k):
        settle(zin.at[k - 8], z_in.at[k - 8])
        total = part[k, :, z].astype(F32) + zin[k - 8].astype(F32)
        zsum[k - 8] = total.astype(BF16)

    def arrivals(k, step):
        return (far_in, near_in, near_in, last_in)[step].at[k]

    def send_up(k, step):
        if k >= 8:
            pair = (
                (zsum.at[k - 8, far, low], z_pass_up.at[k - 8]),
                (zsum.at[k - 8, up, high], z_from_down.at[k - 8, high]),
                (z_pass_up.at[k - 8], z_from_down.at[k - 8, low]),
            )[step]
        else:
            pair = (
                (part.at[k, far, :, low], pass_up.at[k]),
                (part.at[k, up, :, high], from_down.at[k, :, high]),
                (pass_up.at[k, 1 - z], from_down.at[k, 1 - z, low]),
                (pass_up.at[k, z], from_down.at[k, z, low]),
            )[step]
        return remote(pair[0], pair[1], y_send.at[k // 8], arrivals(k, step), to_up)

    def send_down(k, step):
        if k >= 8:
            pair = (
                (zsum.at[k - 8, far, high], z_pass_down.at[k - 8]),
                (zsum.at[k - 8, down, low], z_from_up.at[k - 8, low]),
                (z_pass_down.at[k - 8], z_from_up.at[k - 8, high]),
            )[step]
        else:
            pair = (
                (part.at[k, far, :, high], pass_down.at[k]),
                (part.at[k, down, :, low], from_up.at[k, :, low]),
                (pass_down.at[k, 1 - z], from_up.at[k, 1 - z, high]),
                (pass_down.at[k, z], from_up.at[k, z, high]),
            )[step]
        return remote(pair[0], pair[1], y_send.at[k // 8], arrivals(k, step), to_down)

    def begin(k, *which):
        for step in which or (0, 1):
            send_up(k, step).start()
            send_down(k, step).start()

    def pass_on(k):
        settle(z_from_down.at[k - 8] if k >= 8 else from_down.at[k], far_in.at[k])
        if k >= 8:
            total = z_pass_up[k - 8].astype(F32) + zsum[k - 8, up, 0:4].astype(F32)
            z_pass_up[k - 8] = total.astype(BF16)
            send_up(k, 2).start()
            total = z_pass_down[k - 8].astype(F32) + zsum[k - 8, down, 4:8].astype(F32)
            z_pass_down[k - 8] = total.astype(BF16)
            send_down(k, 2).start()
            return
        for zz, step in ((1 - z, 2), (z, 3)):
            total = pass_up[k, zz].astype(F32) + part[k, up, zz, 0:4].astype(F32)
            pass_up[k, zz] = total.astype(BF16)
            send_up(k, step).start()
            total = pass_down[k, zz].astype(F32) + part[k, down, zz, 4:8].astype(F32)
            pass_down[k, zz] = total.astype(BF16)
            send_down(k, step).start()

    def gathered(k):
        settle(from_down.at[0] if k >= 8 else pass_up.at[pl.ds(0, 3)], near_in.at[k])

    def over_z(k):
        gathered(k)
        other = 1 - z
        total = part[k, y, other].astype(F32) + from_down[k, other].astype(F32)
        z_out[k] = (total + from_up[k, other].astype(F32)).astype(BF16)
        z_copy(k).start()

    def group_of(k):
        return 4 if k >= 8 else 2 * c + (k // 2) % 2

    def core_of(k):
        return c if k >= 8 else k % 2

    def half_of(k):
        return k - 8 if k >= 8 else k // 4

    def owner_walk(k, i):
        to_x, to_zh, to_zl = owner(half_of(k), z, i)
        return to_x * 4 + to_zh, to_zl

    def owner_copy(k, i):
        group = group_of(k)
        walk, zl = owner_walk(k, i)
        return remote(
            turned.at[8 * k + i], operator.at[group, a], o_send, o_recv.at[group],
            at(walk, y, zl, core_of(k)),
        )

    def each_owner(k, other, own=None):
        def run(d, _):
            i = (a + d) % 8
            here = jnp.logical_and(owner_walk(k, i)[0] == a, core_of(k) == c)

            @pl.when(jnp.logical_not(here))
            def _():
                other(i)

            if own is not None:

                @pl.when(here)
                def _():
                    own(i)

            return 0

        lax.fori_loop(0, 8, run, 0)

    def deliver(k):
        if k >= 8:
            gathered(k)
            total = zsum[k - 8, y].astype(F32) + z_from_down[k - 8].astype(F32)
            total = total + z_from_up[k - 8].astype(F32)
        else:
            settle(from_down.at[k], last_in.at[k])
            total = part[k, y, z].astype(F32) + from_down[k, z].astype(F32)
            total = total + from_up[k, z].astype(F32) + from_z[k].astype(F32)
        turned[8 * k : 8 * k + 8] = jnp.swapaxes(total, 0, 1).astype(BF16)

        def keep(i):
            operator[group_of(k), a] = turned[8 * k + i]

        each_owner(k, lambda i: owner_copy(k, i).start(), keep)

    multiply(0, 0, 4)
    send_up(0, 0).start()
    send_down(0, 1).start()
    multiply(0, 4, 8)
    send_down(0, 0).start()
    send_up(0, 1).start()
    begin(1)
    start_zh(1)
    multiply_z(0)
    multiply(1, 0, 8)
    pass_on(0)
    begin(2)
    start_back(1)
    pass_on(1)
    begin(3)
    over_z(0)
    shift(1)
    field_arrived(1)
    multiply_z(1)
    pass_on(2)
    multiply(2, 0, 8)
    begin(4)
    over_z(1)
    multiply(3, 0, 8)
    pass_on(3)
    begin(5)
    sum_z(8)
    by_half = [
        jnp.swapaxes(jnp.swapaxes(dj[h], 0, 1).reshape(16, 8, 192), 0, 1) for h in range(2)
    ]
    aux_out[...] = jnp.stack(by_half, axis=1).reshape(256, 192).T
    over_z(2)
    pass_on(4)
    begin(6)
    deliver(0)
    deliver(1)
    over_z(3)
    pass_on(5)
    begin(7)
    deliver(2)
    deliver(3)
    sum_z(9)
    over_z(4)
    pass_on(6)
    deliver(4)
    over_z(5)
    pass_on(7)
    begin(8)
    begin(9)
    deliver(5)
    over_z(6)
    over_z(7)
    pass_on(8)
    deliver(6)
    pass_on(9)
    deliver(7)
    deliver(8)
    deliver(9)

    settle(gsend.at[pl.ds(0, 15)], a_send)
    settle(ct.at[:, :, c], ct_send)
    settle(blocks.at[pl.ds(0, 15)], g_send)
    settle(pb.at[pl.ds(0, 6)], p_send)
    settle(pb.at[pl.ds(0, 6)], q_send)
    settle(pb.at[pl.ds(0, 6)], b_send)
    settle(field.at[0], f_send)
    settle(part.at[pl.ds(0, 6)], y_send.at[0])
    settle(pass_up.at[pl.ds(0, 6)], y_send.at[1])
    settle(from_down, z_send)

    def wait_group(group):
        core = c if group == 4 else group // 2

        @pl.when(core == c)
        def _():
            settle(operator.at[group, pl.ds(0, 15)], o_recv.at[group])

        @pl.when(core != c)
        def _():
            settle(operator.at[group], o_recv.at[group])

    start_low = wv[0].astype(BF16)
    for group in (0, 2, 1, 3, 4):
        wait_group(group)
        rows = operator[group].reshape(128, 640)
        value = jnp.dot(rows, start_low, preferred_element_type=F32)
        term1[:, group] = value.reshape(16, 8, 128)
    settle(turned.at[pl.ds(0, 77)], o_send)
    matrix = jnp.swapaxes(operator[...], 0, 1).reshape(640, 640)
    term = term1[...].reshape(640, 128)
    total = wv[0] + term
    for degree in range(2, 5):
        term = jnp.dot(matrix, term.astype(BF16), preferred_element_type=F32) * (1.0 / degree)
        total = total + term
    out[0] = total


def hand_over(walkers_in, aux_in, walkers_out, aux_out):
    walkers_out[...] = walkers_in[...]
    aux_out[...] = aux_in[...]


def shape(*dims, dtype=BF16):
    return jax.ShapeDtypeStruct(dims, dtype)


def room(*dims, dtype=BF16):
    return pltpu.VMEM(dims, dtype)


def dma(*dims):
    return pltpu.SemaphoreType.DMA(dims)


def body(walkers, intersection_inverse, aux_draws, chol_half, chol_full):
    new_walkers, aux = pl.pallas_call(
        kernel,
        out_shape=(shape(1, 640, 128, dtype=F32), shape(192, 256, dtype=F32)),
        in_specs=[ANY] * 5,
        out_specs=(VMEM, VMEM),
        scratch_shapes=[
            room(1, 640, 128, dtype=F32),
            room(1, 128, 128, dtype=F32),
            room(192, 256, dtype=F32),
            room(192, 40, 128),
            room(192, 40, 640),
            room(16, 40, 128),
            room(16, 2, 8, 40, 128),
            room(2, 40, 8, 16, 128),
            room(40, 192, 128),
            room(3, 8, 2, 192, 640),
            room(2, 8, 192, 640),
            room(2, 64, 64),
            room(2, 2, 8, 8, 192, dtype=F32),
            room(8, 32, 192),
            room(2, 4, 32, 192),
            room(2, 4, 32, 192),
            room(2, 4, 32, 192),
            room(2, 2, 2, 64, 192),
            room(10, 4, 2, 8, 8, 640),
            room(8, 2, 4, 8, 640),
            room(8, 2, 4, 8, 640),
            room(8, 2, 8, 8, 640),
            room(8, 2, 8, 8, 640),
            room(8, 8, 8, 640),
            room(8, 8, 8, 640),
            room(2, 4, 8, 8, 640),
            room(2, 4, 8, 8, 640),
            room(2, 4, 8, 640),
            room(2, 4, 8, 640),
            room(2, 8, 8, 640),
            room(2, 8, 8, 640),
            room(80, 8, 640),
            room(5, 16, 8, 640),
            room(16, 5, 8, 128, dtype=F32),
            dma(5), dma(), dma(), dma(), dma(2), dma(), dma(2, 8), dma(), dma(2), dma(), dma(2),
            dma(), dma(2), dma(), dma(2), dma(2), dma(10), dma(10), dma(8), dma(), dma(2), dma(), dma(5),
        ],
        compiler_params=pltpu.CompilerParams(
            collective_id=0, has_side_effects=True, vmem_limit_bytes=54 * 2**20
        ),
        name="propagate",
    )(walkers, intersection_inverse, aux_draws.T, chol_half, chol_full)
    new_walkers, aux = pl.pallas_call(
        hand_over,
        out_shape=(shape(1, 640, 128, dtype=F32), shape(192, 256, dtype=F32)),
        in_specs=[VMEM] * 2,
        out_specs=(VMEM, VMEM),
        name="hand_over",
    )(new_walkers, aux)
    return new_walkers, aux.T


def solution(mesh):
    placed = (
        P(("walk", "chol"), None, None),
        P(("walk", "chol"), None, None),
        P(None, "chol"),
        P("chol", "walk", None),
        P("chol", "walk", None),
    )
    return jax.shard_map(
        body,
        mesh=mesh,
        in_specs=placed,
        out_specs=(P(("walk", "chol"), None, None), P(None, "chol")),
        check_vma=False,
    )
```

```python
import jax
import jax.numpy as jnp
from jax import lax
from jax.experimental import pallas as pl
from jax.experimental.pallas import tpu as pltpu
from jax.sharding import PartitionSpec as P

MESH = pl.DeviceIdType.MESH
BF16 = jnp.bfloat16
F32 = jnp.float32
ANY = pl.BlockSpec(memory_space=pl.ANY)
VMEM = pl.BlockSpec(memory_space=pltpu.VMEM)


def place():
    a = lax.axis_index("walk")
    b = lax.axis_index("chol")
    return a, b // 4, (b // 2) % 2, b % 2


def at(a, y, z, c):
    return (a, y * 4 + z * 2 + c)


def remote(src, dst, send, recv, target):
    return pltpu.make_async_remote_copy(
        src_ref=src, dst_ref=dst, send_sem=send, recv_sem=recv, device_id=target, device_id_type=MESH
    )


def settle(ref, sem):
    a, y, z, c = place()
    remote(ref, ref, sem, sem, at(a, y, z, 1 - c)).wait_recv()


def greet(target):
    pl.semaphore_signal(pltpu.get_barrier_semaphore(), inc=1, device_id=target, device_id_type=MESH)


def kernel(
    walkers, inverse, draws, half, full,
    out, aux_out,
    wv, iv, dv, hv, fv, gsend, blocks, gt, ht, htk, ct, given, order, dj, pb, xin, zhin, ball, field,
    part, pass_up, pass_down, from_down, from_up, z_out, from_z,
    zin, zsum, z_pass_up, z_pass_down, z_from_down, z_from_up, turned, operator, term1,
    in_sem, ct_send, ct_recv, a_send, a_recv, g_send, g_recv, p_send, p_recv, q_send, q_recv,
    b_send, b_recv, f_send, f_recv, y_send, far_in, near_in, last_in, z_send, z_in, o_send, o_recv,
):
    a, y, z, c = place()
    x, zh = a // 4, a % 4
    up, down, far = (y + 1) % 4, (y + 3) % 4, (y + 2) % 4
    to_up, to_down, to_z = at(a, up, z, c), at(a, down, z, c), at(a, y, 1 - z, c)
    sibling = at(a, y, z, 1 - c)

    def load(index):
        pair = ((walkers, wv), (inverse, iv), (half, hv), (full, fv), (draws, dv))[index]
        return pltpu.make_async_copy(pair[0], pair[1], in_sem.at[index])

    for index in range(5):
        load(index).start()

    def greet_walk(d, _):
        greet(at((a + d) % 16, y, z, c))
        return 0

    lax.fori_loop(1, 16, greet_walk, 0)

    def greet_senders(d, _):
        xx, core = d // 2, d % 2

        @pl.when(jnp.logical_or(xx != x, core != c))
        def _():
            greet(at(xx * 4 + zh, y, z, core))

        greet(at(xx * 4 + (zh + 2) % 4, y, 1 - z, core))
        greet(at(xx * 4 + (zh + 3) % 4, y, 1, core))
        greet(at(xx * 4 + (zh + 1) % 4, y, 0, core))
        return 0

    lax.fori_loop(0, 8, greet_senders, 0)
    to_far = at(a, far, z, c)
    for target in (to_far, to_up, to_down, to_z, sibling):
        greet(target)

    load(0).wait()
    load(1).wait()
    green = jnp.dot(
        wv[0], iv[0], precision=lax.Precision.HIGHEST, preferred_element_type=F32
    ).astype(BF16)
    gsend[...] = green.reshape(16, 40, 128)
    pl.semaphore_wait(pltpu.get_barrier_semaphore(), 51)

    def each_other(step):
        def run(d, _):
            step(d)
            return 0

        lax.fori_loop(1, 16, run, 0)

    def peer(d):
        return (a + d) % 16

    def slot(yy, zz):
        return c * 8 + yy * 2 + zz

    own = slot(y, z)

    def green_copy(to):
        return remote(
            gsend.at[to], blocks.at[own, a % 2, a // 2], a_send, a_recv.at[a % 2], at(to, y, z, c)
        )

    @pl.when(a % 2 == 0)
    def _():
        each_other(lambda d: green_copy(peer(d)).start())

    blocks[own, a % 2, a // 2] = gsend[a]

    load(2).wait()

    def turn_half(i, _):
        n0 = pl.multiple_of(i * 16, 16)
        ht[:, pl.ds(n0, 16), :] = jnp.swapaxes(hv[pl.ds(n0, 16)], 0, 1)
        return 0

    lax.fori_loop(0, 12, turn_half, 0)

    load(3).wait()

    def turn_full(group, target):
        def turn(i, _):
            n0 = pl.multiple_of(i * 16, 16)
            target[:, pl.ds(n0, 16), :] = jnp.swapaxes(
                fv[pl.ds(n0, 16), group * 8 : group * 8 + 8, :], 0, 1
            )
            return 0

        lax.fori_loop(0, 12, turn, 0)

    def turn_given(i):
        for core in range(2):

            @pl.when(c == core)
            def _(core=core):
                turn_full(2 * (1 - core) + i, given.at[i])

    def turn_kept(i):
        for core in range(2):

            @pl.when(c == core)
            def _(core=core):
                turn_full(2 * core + i, ct.at[i, :, core])

    def give(i):
        source = ct.at[2, :, c] if i == 2 else given.at[i]
        return remote(source, ct.at[i, :, c], ct_send, ct_recv, sibling)

    turn_given(0)
    give(0).start()
    turn_given(1)
    give(1).start()
    for core in range(2):

        @pl.when(c == core)
        def _(core=core):
            turn_full(4, ct.at[2, :, core])

    give(2).start()

    @pl.when(a % 2 == 1)
    def _():
        each_other(lambda d: green_copy(peer(d)).start())

    turn_kept(0)
    turn_kept(1)

    def owner(h, zl, i):
        same = 1 - (zh + h) % 2
        pick = i % 2
        to_zh = (zh + same * 2 * pick + (1 - same) * (3 - 2 * zl)) % 4
        return i // 2, to_zh, same * ((zl + pick) % 2) + (1 - same) * pick

    for h in range(2):
        row = lax.broadcasted_iota(jnp.int32, (64, 64), 0)
        column = lax.broadcasted_iota(jnp.int32, (64, 64), 1)
        to_x, to_zh, to_zl = owner(h, (row // 8) % 2, row % 8)
        source = (row // 16) * 16 + to_zl * 8 + to_x * 2 + to_zh // 2
        order[h] = jnp.where(source == column, 1.0, 0.0).astype(BF16)

    load(4).wait()
    by_walker = dv[...].T.reshape(8, 2, 16, 192)
    for h in range(2):
        half_draws = jnp.swapaxes(by_walker[:, h], 0, 1).reshape(8, 2, 8, 192)
        for core in range(2):
            dj[h, core] = half_draws[:, core]

    def wait_green(h):
        @pl.when(a % 2 == h)
        def _():
            settle(blocks.at[0, h, pl.ds(0, 7)], a_recv.at[h])

        @pl.when(a % 2 != h)
        def _():
            settle(blocks.at[0, h], a_recv.at[h])

    def spread(h, index):
        yy, zz, target = (
            (y, z, to_far), (y, z, to_up), (y, z, to_down), (y, z, to_z), (y, z, sibling),
            (y, 1 - z, to_up), (y, 1 - z, to_down), (far, z, to_z),
            (y, 1 - z, sibling), (far, z, sibling), (down, z, sibling), (up, z, sibling),
            (down, 1 - z, sibling), (up, 1 - z, sibling), (far, 1 - z, sibling),
        )[index]
        ref = blocks.at[slot(yy, zz), h]
        return remote(ref, ref, g_send, g_recv.at[h, index if index < 8 else 4], target)

    def start(h, *indices):
        for index in indices:
            spread(h, index).start()

    def landed(h, index):
        settle(blocks.at[0, h], g_recv.at[h, index])

    def spread_own(h):
        start(h, 3, 0, 1, 2, 4)

    def spread_second(h):
        landed(h, 3)
        start(h, 5, 6, 8)
        landed(h, 0)
        start(h, 7, 9)

    def spread_on(h):
        for index in (1, 2, 5, 6, 7):
            landed(h, index)
            start(h, {1: 10, 2: 11, 5: 12, 6: 13, 7: 14}[index])
        settle(blocks.at[pl.ds(0, 4)], g_recv.at[h, 4])

    def bias_sums(h):
        def turn(i, _):
            both = blocks[pl.ds(2 * i, 2), h].reshape(16, 40, 128)
            gt[h, :, i] = jnp.swapaxes(both, 0, 1)
            return 0

        lax.fori_loop(0, 8, turn, 0)

        def step(i, acc):
            p0 = i * 8
            left = jnp.concatenate([gt[h, p0 + q].reshape(128, 128) for q in range(8)], axis=1)
            right = htk[pl.ds(p0, 8)].reshape(1024, 192)
            return acc + jnp.dot(left, right, preferred_element_type=F32)

        partial = lax.fori_loop(0, 5, step, jnp.zeros((128, 192), F32))
        pb[4 * h : 4 * h + 4] = partial.astype(BF16).reshape(4, 32, 192)

    def x_peer(e):
        return (x + e) % 4

    def x_copy(h, e):
        return remote(
            pb.at[4 * h + x_peer(e)], xin.at[h, x], p_send, p_recv.at[h],
            at(x_peer(e) * 4 + zh, y, z, c),
        )

    def zh_copy(h, e):
        ref = zhin.at[h, zh]
        return remote(ref, ref, q_send, q_recv.at[h], at(x * 4 + (zh + e) % 4, y, z, c))

    def back_copy(h, e):
        ref = ball.at[h, x]
        return remote(ref, ref, b_send, b_recv.at[h], at(x_peer(e) * 4 + zh, y, z, c))

    def start_x(h):
        for e in (2, 1, 3):
            x_copy(h, e).start()
        xin[h, x] = pb[4 * h + x]

    def start_zh(h):
        settle(xin.at[h, pl.ds(0, 3)], p_recv.at[h])
        zhin[h, zh] = jnp.sum(xin[h].astype(F32), axis=0).astype(BF16)
        for e in (2, 1, 3):
            zh_copy(h, e).start()

    def start_back(h):
        settle(zhin.at[h, pl.ds(0, 3)], q_recv.at[h])
        ball[h, x] = jnp.sum(zhin[h].astype(F32), axis=0).astype(BF16)
        for e in (2, 1, 3):
            back_copy(h, e).start()

    def field_copy(h):
        ref = field.at[c, h]
        return remote(ref, ref, f_send, f_recv.at[h], sibling)

    def field_arrived(h):
        settle(field.at[0, h], f_recv.at[h])

    def shift(h):
        settle(ball.at[h, pl.ds(0, 3)], b_recv.at[h])
        shifted = dj[h] - ball[h].astype(F32).reshape(2, 8, 8, 192)
        dj[h] = shifted
        for core in range(2):
            rows = shifted[core].astype(BF16).reshape(64, 192)
            rows = jnp.dot(order[h], rows, preferred_element_type=F32)
            field[c, h, core] = rows.astype(BF16)
        field_copy(h).start()

    def turn_columns(i, _):
        for q in range(4):
            htk[4 * i + q] = ht[4 * i + q].astype(F32).T.astype(BF16)
        return 0

    wait_green(0)
    spread_own(0)
    lax.fori_loop(0, 5, turn_columns, 0)
    spread_second(0)
    wait_green(1)
    spread_own(1)
    lax.fori_loop(5, 10, turn_columns, 0)
    spread_on(0)
    bias_sums(0)
    start_x(0)
    spread_second(1)
    start_zh(0)
    spread_on(1)
    start_back(0)
    bias_sums(1)
    start_x(1)
    shift(0)

    low, high = pl.ds(0, 4), pl.ds(4, 4)

    def multiply(pair, first_row=0, last_row=8):
        left = [field[s, pair // 2].reshape(128, 192) for s in range(2)]

        def row(r, _):
            value = jnp.dot(left[0], ct[pair % 2, r, 0], preferred_element_type=F32)
            value = value + jnp.dot(left[1], ct[pair % 2, r, 1], preferred_element_type=F32)
            value = value.astype(BF16).reshape(2, 4, 2, 8, 640)
            for core in range(2):
                part[2 * pair + core, :, :, r] = value[core]
            return 0

        lax.fori_loop(first_row, last_row, row, 0)

    def multiply_z(h):
        left = [field[s, h, c] for s in range(2)]

        def row(r, _):
            value = jnp.dot(left[0], ct[2, r, 0], preferred_element_type=F32)
            value = value + jnp.dot(left[1], ct[2, r, 1], preferred_element_type=F32)
            part[8 + h, :, :, r] = value.astype(BF16).reshape(4, 2, 8, 640)
            return 0

        for rows in (low, high):
            lax.fori_loop(rows.start, rows.start + 4, row, 0)
            z_first(8 + h, rows).start()

    def z_first(k, rows):
        return remote(
            part.at[k, :, 1 - z, rows], zin.at[k - 8, :, rows], z_send, z_in.at[k - 8], to_z
        )

    def z_copy(k):
        return remote(z_out.at[k], from_z.at[k], z_send, last_in.at[k], to_z)

    def sum_z(k):
        settle(zin.at[k - 8], z_in.at[k - 8])
        total = part[k, :, z].astype(F32) + zin[k - 8].astype(F32)
        zsum[k - 8] = total.astype(BF16)

    def arrivals(k, step):
        return (far_in, near_in, near_in, last_in)[step].at[k]

    def send_up(k, step):
        if k >= 8:
            pair = (
                (zsum.at[k - 8, far, low], z_pass_up.at[k - 8]),
                (zsum.at[k - 8, up, high], z_from_down.at[k - 8, high]),
                (z_pass_up.at[k - 8], z_from_down.at[k - 8, low]),
            )[step]
        else:
            pair = (
                (part.at[k, far, :, low], pass_up.at[k]),
                (part.at[k, up, :, high], from_down.at[k, :, high]),
                (pass_up.at[k, 1 - z], from_down.at[k, 1 - z, low]),
                (pass_up.at[k, z], from_down.at[k, z, low]),
            )[step]
        return remote(pair[0], pair[1], y_send.at[k // 8], arrivals(k, step), to_up)

    def send_down(k, step):
        if k >= 8:
            pair = (
                (zsum.at[k - 8, far, high], z_pass_down.at[k - 8]),
                (zsum.at[k - 8, down, low], z_from_up.at[k - 8, low]),
                (z_pass_down.at[k - 8], z_from_up.at[k - 8, high]),
            )[step]
        else:
            pair = (
                (part.at[k, far, :, high], pass_down.at[k]),
                (part.at[k, down, :, low], from_up.at[k, :, low]),
                (pass_down.at[k, 1 - z], from_up.at[k, 1 - z, high]),
                (pass_down.at[k, z], from_up.at[k, z, high]),
            )[step]
        return remote(pair[0], pair[1], y_send.at[k // 8], arrivals(k, step), to_down)

    def begin(k, *which):
        for step in which or (0, 1):
            send_up(k, step).start()
            send_down(k, step).start()

    def pass_on(k):
        settle(z_from_down.at[k - 8] if k >= 8 else from_down.at[k], far_in.at[k])
        if k >= 8:
            total = z_pass_up[k - 8].astype(F32) + zsum[k - 8, up, 0:4].astype(F32)
            z_pass_up[k - 8] = total.astype(BF16)
            send_up(k, 2).start()
            total = z_pass_down[k - 8].astype(F32) + zsum[k - 8, down, 4:8].astype(F32)
            z_pass_down[k - 8] = total.astype(BF16)
            send_down(k, 2).start()
            return
        for zz, step in ((1 - z, 2), (z, 3)):
            total = pass_up[k, zz].astype(F32) + part[k, up, zz, 0:4].astype(F32)
            pass_up[k, zz] = total.astype(BF16)
            send_up(k, step).start()
            total = pass_down[k, zz].astype(F32) + part[k, down, zz, 4:8].astype(F32)
            pass_down[k, zz] = total.astype(BF16)
            send_down(k, step).start()

    def gathered(k):
        settle(from_down.at[0] if k >= 8 else pass_up.at[pl.ds(0, 3)], near_in.at[k])

    def over_z(k):
        gathered(k)
        other = 1 - z
        total = part[k, y, other].astype(F32) + from_down[k, other].astype(F32)
        z_out[k] = (total + from_up[k, other].astype(F32)).astype(BF16)
        z_copy(k).start()

    def group_of(k):
        return 4 if k >= 8 else 2 * c + (k // 2) % 2

    def core_of(k):
        return c if k >= 8 else k % 2

    def half_of(k):
        return k - 8 if k >= 8 else k // 4

    def owner_walk(k, i):
        to_x, to_zh, to_zl = owner(half_of(k), z, i)
        return to_x * 4 + to_zh, to_zl

    def owner_copy(k, i):
        group = group_of(k)
        walk, zl = owner_walk(k, i)
        return remote(
            turned.at[8 * k + i], operator.at[group, a], o_send, o_recv.at[group],
            at(walk, y, zl, core_of(k)),
        )

    def each_owner(k, other, own=None):
        def run(d, _):
            turn = d // 2
            away = jnp.where(turn < 2, 2 + turn, 3 - turn)
            i = ((x + away) % 4) * 2 + 1 - d % 2
            here = jnp.logical_and(owner_walk(k, i)[0] == a, core_of(k) == c)

            @pl.when(jnp.logical_not(here))
            def _():
                other(i)

            if own is not None:

                @pl.when(here)
                def _():
                    own(i)

            return 0

        lax.fori_loop(0, 8, run, 0)

    def deliver(k):
        if k >= 8:
            gathered(k)
            total = zsum[k - 8, y].astype(F32) + z_from_down[k - 8].astype(F32)
            total = total + z_from_up[k - 8].astype(F32)
        else:
            settle(from_down.at[k], last_in.at[k])
            total = part[k, y, z].astype(F32) + from_down[k, z].astype(F32)
            total = total + from_up[k, z].astype(F32) + from_z[k].astype(F32)
        turned[8 * k : 8 * k + 8] = jnp.swapaxes(total, 0, 1).astype(BF16)

        def keep(i):
            operator[group_of(k), a] = turned[8 * k + i]

        each_owner(k, lambda i: owner_copy(k, i).start(), keep)

    settle(ct.at[:, :, 1 - c], ct_recv)
    field_arrived(0)
    multiply(0, 0, 4)
    send_up(0, 0).start()
    send_down(0, 1).start()
    multiply(0, 4, 8)
    send_down(0, 0).start()
    send_up(0, 1).start()
    begin(1)
    start_zh(1)
    multiply_z(0)
    multiply(1)
    pass_on(0)
    begin(2)
    start_back(1)
    pass_on(1)
    begin(3)
    shift(1)
    over_z(0)
    field_arrived(1)
    multiply_z(1)
    pass_on(2)
    multiply(2)
    begin(4)
    over_z(1)
    multiply(3)
    pass_on(3)
    begin(5)
    sum_z(8)
    by_half = [
        jnp.swapaxes(jnp.swapaxes(dj[h], 0, 1).reshape(16, 8, 192), 0, 1) for h in range(2)
    ]
    aux_out[...] = jnp.stack(by_half, axis=1).reshape(256, 192).T
    over_z(2)
    pass_on(4)
    begin(6)
    deliver(0)
    deliver(1)
    over_z(3)
    pass_on(5)
    begin(7)
    deliver(2)
    deliver(3)
    sum_z(9)
    over_z(4)
    pass_on(6)
    deliver(4)
    over_z(5)
    pass_on(7)
    begin(8)
    begin(9)
    deliver(5)
    over_z(6)
    over_z(7)
    pass_on(8)
    deliver(6)
    pass_on(9)
    deliver(7)
    deliver(8)
    deliver(9)

    settle(gsend.at[pl.ds(0, 15)], a_send)
    settle(ct.at[:, :, c], ct_send)
    settle(blocks.at[pl.ds(0, 15)], g_send)
    settle(pb.at[pl.ds(0, 6)], p_send)
    settle(pb.at[pl.ds(0, 6)], q_send)
    settle(pb.at[pl.ds(0, 6)], b_send)
    settle(field.at[0], f_send)
    settle(part.at[pl.ds(0, 6)], y_send.at[0])
    settle(pass_up.at[pl.ds(0, 6)], y_send.at[1])
    settle(from_down, z_send)

    def wait_group(group):
        core = c if group == 4 else group // 2

        @pl.when(core == c)
        def _():
            settle(operator.at[group, pl.ds(0, 15)], o_recv.at[group])

        @pl.when(core != c)
        def _():
            settle(operator.at[group], o_recv.at[group])

    start_low = wv[0].astype(BF16)
    for group in (0, 2, 1, 3, 4):
        wait_group(group)
        rows = operator[group].reshape(128, 640)
        value = jnp.dot(rows, start_low, preferred_element_type=F32)
        term1[:, group] = value.reshape(16, 8, 128)
    settle(turned.at[pl.ds(0, 77)], o_send)
    matrix = jnp.swapaxes(operator[...], 0, 1).reshape(640, 640)
    term = term1[...].reshape(640, 128)
    total = wv[0] + term
    for degree in range(2, 5):
        term = jnp.dot(matrix, term.astype(BF16), preferred_element_type=F32) * (1.0 / degree)
        total = total + term
    out[0] = total


def hand_over(walkers_in, aux_in, walkers_out, aux_out):
    walkers_out[...] = walkers_in[...]
    aux_out[...] = aux_in[...]


def shape(*dims, dtype=BF16):
    return jax.ShapeDtypeStruct(dims, dtype)


def room(*dims, dtype=BF16):
    return pltpu.VMEM(dims, dtype)


def dma(*dims):
    return pltpu.SemaphoreType.DMA(dims)


def body(walkers, intersection_inverse, aux_draws, chol_half, chol_full):
    new_walkers, aux = pl.pallas_call(
        kernel,
        out_shape=(shape(1, 640, 128, dtype=F32), shape(192, 256, dtype=F32)),
        in_specs=[ANY] * 5,
        out_specs=(VMEM, VMEM),
        scratch_shapes=[
            room(1, 640, 128, dtype=F32),
            room(1, 128, 128, dtype=F32),
            room(192, 256, dtype=F32),
            room(192, 40, 128),
            room(192, 40, 640),
            room(16, 40, 128),
            room(16, 2, 8, 40, 128),
            room(2, 40, 8, 16, 128),
            room(40, 192, 128),
            room(40, 128, 192),
            room(3, 8, 2, 192, 640),
            room(2, 8, 192, 640),
            room(2, 64, 64),
            room(2, 2, 8, 8, 192, dtype=F32),
            room(8, 32, 192),
            room(2, 4, 32, 192),
            room(2, 4, 32, 192),
            room(2, 4, 32, 192),
            room(2, 2, 2, 64, 192),
            room(10, 4, 2, 8, 8, 640),
            room(8, 2, 4, 8, 640),
            room(8, 2, 4, 8, 640),
            room(8, 2, 8, 8, 640),
            room(8, 2, 8, 8, 640),
            room(8, 8, 8, 640),
            room(8, 8, 8, 640),
            room(2, 4, 8, 8, 640),
            room(2, 4, 8, 8, 640),
            room(2, 4, 8, 640),
            room(2, 4, 8, 640),
            room(2, 8, 8, 640),
            room(2, 8, 8, 640),
            room(80, 8, 640),
            room(5, 16, 8, 640),
            room(16, 5, 8, 128, dtype=F32),
            dma(5), dma(), dma(), dma(), dma(2), dma(), dma(2, 8), dma(), dma(2), dma(), dma(2),
            dma(), dma(2), dma(), dma(2), dma(2), dma(10), dma(10), dma(8), dma(), dma(2), dma(), dma(5),
        ],
        compiler_params=pltpu.CompilerParams(
            collective_id=0, has_side_effects=True, vmem_limit_bytes=56 * 2**20
        ),
        name="propagate",
    )(walkers, intersection_inverse, aux_draws.T, chol_half, chol_full)
    new_walkers, aux = pl.pallas_call(
        hand_over,
        out_shape=(shape(1, 640, 128, dtype=F32), shape(192, 256, dtype=F32)),
        in_specs=[VMEM] * 2,
        out_specs=(VMEM, VMEM),
        name="hand_over",
    )(new_walkers, aux)
    return new_walkers, aux.T


def solution(mesh):
    placed = (
        P(("walk", "chol"), None, None),
        P(("walk", "chol"), None, None),
        P(None, "chol"),
        P("chol", "walk", None),
        P("chol", "walk", None),
    )
    return jax.shard_map(
        body,
        mesh=mesh,
        in_specs=placed,
        out_specs=(P(("walk", "chol"), None, None), P(None, "chol")),
        check_vma=False,
    )
```

```python
import jax
import jax.numpy as jnp
from jax import lax
from jax.experimental import pallas as pl
from jax.experimental.pallas import tpu as pltpu
from jax.sharding import PartitionSpec as P

MESH = pl.DeviceIdType.MESH
BF16 = jnp.bfloat16
F32 = jnp.float32
ANY = pl.BlockSpec(memory_space=pl.ANY)
VMEM = pl.BlockSpec(memory_space=pltpu.VMEM)


def place():
    a = lax.axis_index("walk")
    b = lax.axis_index("chol")
    return a, b // 4, (b // 2) % 2, b % 2


def at(a, y, z, c):
    return (a, y * 4 + z * 2 + c)


def remote(src, dst, send, recv, target):
    return pltpu.make_async_remote_copy(
        src_ref=src, dst_ref=dst, send_sem=send, recv_sem=recv, device_id=target, device_id_type=MESH
    )


def settle(ref, sem):
    a, y, z, c = place()
    remote(ref, ref, sem, sem, at(a, y, z, 1 - c)).wait_recv()


def greet(target):
    pl.semaphore_signal(pltpu.get_barrier_semaphore(), inc=1, device_id=target, device_id_type=MESH)


def kernel(
    walkers, inverse, draws, half, full,
    out, aux_out,
    wv, iv, dv, hv, fv, gsend, blocks, gt, ht, htk, ct, given, order, dj, pb, xin, zhin, ball, field,
    part, pass_up, pass_down, from_down, from_up, z_out, from_z,
    zin, zsum, z_pass_up, z_pass_down, z_from_down, z_from_up, turned, operator, term1,
    in_sem, ct_send, ct_recv, a_send, a_recv, g_send, g_recv, p_send, p_recv, q_send, q_recv,
    b_send, b_recv, f_send, f_recv, y_send, far_in, near_in, last_in, z_send, z_in, o_send, o_recv,
):
    a, y, z, c = place()
    x, zh = a // 4, a % 4
    up, down, far = (y + 1) % 4, (y + 3) % 4, (y + 2) % 4
    to_up, to_down, to_z = at(a, up, z, c), at(a, down, z, c), at(a, y, 1 - z, c)
    sibling = at(a, y, z, 1 - c)

    def load(index):
        pair = ((walkers, wv), (inverse, iv), (half, hv), (full, fv), (draws, dv))[index]
        return pltpu.make_async_copy(pair[0], pair[1], in_sem.at[index])

    def greet_walk(d, _):
        greet(at((a + d) % 16, y, z, c))
        return 0

    lax.fori_loop(1, 16, greet_walk, 0)

    def greet_senders(d, _):
        xx, core = d // 2, d % 2

        @pl.when(jnp.logical_or(xx != x, core != c))
        def _():
            greet(at(xx * 4 + zh, y, z, core))

        greet(at(xx * 4 + (zh + 2) % 4, y, 1 - z, core))
        greet(at(xx * 4 + (zh + 3) % 4, y, 1, core))
        greet(at(xx * 4 + (zh + 1) % 4, y, 0, core))
        return 0

    lax.fori_loop(0, 8, greet_senders, 0)
    to_far = at(a, far, z, c)
    for target in (to_far, to_up, to_down, to_z, sibling):
        greet(target)

    for index in range(5):
        load(index).start()

    load(0).wait()
    load(1).wait()
    green = jnp.dot(
        wv[0], iv[0], precision=lax.Precision.HIGHEST, preferred_element_type=F32
    ).astype(BF16)
    gsend[...] = green.reshape(16, 40, 128)
    pl.semaphore_wait(pltpu.get_barrier_semaphore(), 51)

    def each_other(step):
        def run(d, _):
            step(d)
            return 0

        lax.fori_loop(1, 16, run, 0)

    def away(n):
        return jnp.where(n < 2, 2 + n, 3 - n)

    def peer(d):
        n = d - 1
        return ((x + away(n % 4)) % 4) * 4 + (zh + away(n // 4)) % 4

    def slot(yy, zz):
        return c * 8 + yy * 2 + zz

    own = slot(y, z)

    def green_copy(to):
        return remote(
            gsend.at[to], blocks.at[own, a % 2, a // 2], a_send, a_recv.at[a % 2], at(to, y, z, c)
        )

    @pl.when(a % 2 == 0)
    def _():
        each_other(lambda d: green_copy(peer(d)).start())

    blocks[own, a % 2, a // 2] = gsend[a]

    load(2).wait()

    def turn_half(i, _):
        n0 = pl.multiple_of(i * 16, 16)
        ht[:, pl.ds(n0, 16), :] = jnp.swapaxes(hv[pl.ds(n0, 16)], 0, 1)
        return 0

    lax.fori_loop(0, 12, turn_half, 0)

    load(3).wait()

    def turn_full(group, target):
        def turn(i, _):
            n0 = pl.multiple_of(i * 16, 16)
            target[:, pl.ds(n0, 16), :] = jnp.swapaxes(
                fv[pl.ds(n0, 16), group * 8 : group * 8 + 8, :], 0, 1
            )
            return 0

        lax.fori_loop(0, 12, turn, 0)

    def turn_given(i):
        for core in range(2):

            @pl.when(c == core)
            def _(core=core):
                turn_full(2 * (1 - core) + i, given.at[i])

    def turn_kept(i):
        for core in range(2):

            @pl.when(c == core)
            def _(core=core):
                turn_full(2 * core + i, ct.at[i, :, core])

    def give(i):
        source = ct.at[2, :, c] if i == 2 else given.at[i]
        return remote(source, ct.at[i, :, c], ct_send, ct_recv, sibling)

    turn_given(0)
    give(0).start()
    turn_given(1)
    give(1).start()
    for core in range(2):

        @pl.when(c == core)
        def _(core=core):
            turn_full(4, ct.at[2, :, core])

    give(2).start()

    @pl.when(a % 2 == 1)
    def _():
        each_other(lambda d: green_copy(peer(d)).start())

    turn_kept(0)
    turn_kept(1)

    def owner(h, zl, i):
        same = 1 - (zh + h) % 2
        pick = i % 2
        to_zh = (zh + same * 2 * pick + (1 - same) * (3 - 2 * zl)) % 4
        return i // 2, to_zh, same * ((zl + pick) % 2) + (1 - same) * pick

    for h in range(2):
        row = lax.broadcasted_iota(jnp.int32, (64, 64), 0)
        column = lax.broadcasted_iota(jnp.int32, (64, 64), 1)
        to_x, to_zh, to_zl = owner(h, (row // 8) % 2, row % 8)
        source = (row // 16) * 16 + to_zl * 8 + to_x * 2 + to_zh // 2
        order[h] = jnp.where(source == column, 1.0, 0.0).astype(BF16)

    load(4).wait()
    by_walker = dv[...].T.reshape(8, 2, 16, 192)
    for h in range(2):
        half_draws = jnp.swapaxes(by_walker[:, h], 0, 1).reshape(8, 2, 8, 192)
        for core in range(2):
            dj[h, core] = half_draws[:, core]

    def wait_green(h):
        @pl.when(a % 2 == h)
        def _():
            settle(blocks.at[0, h, pl.ds(0, 7)], a_recv.at[h])

        @pl.when(a % 2 != h)
        def _():
            settle(blocks.at[0, h], a_recv.at[h])

    def spread(h, index):
        yy, zz, target = (
            (y, z, to_far), (y, z, to_up), (y, z, to_down), (y, z, to_z), (y, z, sibling),
            (y, 1 - z, to_up), (y, 1 - z, to_down), (far, z, to_z),
            (y, 1 - z, sibling), (far, z, sibling), (down, z, sibling), (up, z, sibling),
            (down, 1 - z, sibling), (up, 1 - z, sibling), (far, 1 - z, sibling),
        )[index]
        ref = blocks.at[slot(yy, zz), h]
        return remote(ref, ref, g_send, g_recv.at[h, index if index < 8 else 4], target)

    def start(h, *indices):
        for index in indices:
            spread(h, index).start()

    def landed(h, index):
        settle(blocks.at[0, h], g_recv.at[h, index])

    def spread_own(h):
        start(h, 3, 0, 1, 2, 4)

    def spread_second(h):
        landed(h, 3)
        start(h, 5, 6, 8)
        landed(h, 0)
        start(h, 7, 9)

    def spread_on(h):
        for index in (1, 2, 5, 6, 7):
            landed(h, index)
            start(h, {1: 10, 2: 11, 5: 12, 6: 13, 7: 14}[index])
        settle(blocks.at[pl.ds(0, 4)], g_recv.at[h, 4])

    def bias_sums(h):
        def turn(i, _):
            both = blocks[pl.ds(2 * i, 2), h].reshape(16, 40, 128)
            gt[h, :, i] = jnp.swapaxes(both, 0, 1)
            return 0

        lax.fori_loop(0, 8, turn, 0)

        def step(i, acc):
            p0 = i * 8
            left = jnp.concatenate([gt[h, p0 + q].reshape(128, 128) for q in range(8)], axis=1)
            right = htk[pl.ds(p0, 8)].reshape(1024, 192)
            return acc + jnp.dot(left, right, preferred_element_type=F32)

        partial = lax.fori_loop(0, 5, step, jnp.zeros((128, 192), F32))
        pb[4 * h : 4 * h + 4] = partial.astype(BF16).reshape(4, 32, 192)

    def x_peer(e):
        return (x + e) % 4

    def x_copy(h, e):
        return remote(
            pb.at[4 * h + x_peer(e)], xin.at[h, x], p_send, p_recv.at[h],
            at(x_peer(e) * 4 + zh, y, z, c),
        )

    def zh_copy(h, e):
        ref = zhin.at[h, zh]
        return remote(ref, ref, q_send, q_recv.at[h], at(x * 4 + (zh + e) % 4, y, z, c))

    def back_copy(h, e):
        ref = ball.at[h, x]
        return remote(ref, ref, b_send, b_recv.at[h], at(x_peer(e) * 4 + zh, y, z, c))

    def start_x(h):
        for e in (2, 1, 3):
            x_copy(h, e).start()
        xin[h, x] = pb[4 * h + x]

    def start_zh(h):
        settle(xin.at[h, pl.ds(0, 3)], p_recv.at[h])
        zhin[h, zh] = jnp.sum(xin[h].astype(F32), axis=0).astype(BF16)
        for e in (2, 1, 3):
            zh_copy(h, e).start()

    def start_back(h):
        settle(zhin.at[h, pl.ds(0, 3)], q_recv.at[h])
        ball[h, x] = jnp.sum(zhin[h].astype(F32), axis=0).astype(BF16)
        for e in (2, 1, 3):
            back_copy(h, e).start()

    def field_copy(h):
        ref = field.at[c, h]
        return remote(ref, ref, f_send, f_recv.at[h], sibling)

    def field_arrived(h):
        settle(field.at[0, h], f_recv.at[h])

    def shift(h):
        settle(ball.at[h, pl.ds(0, 3)], b_recv.at[h])
        shifted = dj[h] - ball[h].astype(F32).reshape(2, 8, 8, 192)
        dj[h] = shifted
        for core in range(2):
            rows = shifted[core].astype(BF16).reshape(64, 192)
            rows = jnp.dot(order[h], rows, preferred_element_type=F32)
            field[c, h, core] = rows.astype(BF16)
        field_copy(h).start()

    def turn_columns(i, _):
        for q in range(4):
            htk[4 * i + q] = ht[4 * i + q].astype(F32).T.astype(BF16)
        return 0

    wait_green(0)
    spread_own(0)
    lax.fori_loop(0, 5, turn_columns, 0)
    spread_second(0)
    wait_green(1)
    spread_own(1)
    lax.fori_loop(5, 10, turn_columns, 0)
    spread_on(0)
    bias_sums(0)
    start_x(0)
    spread_second(1)
    start_zh(0)
    spread_on(1)
    start_back(0)
    bias_sums(1)
    start_x(1)
    shift(0)

    low, high = pl.ds(0, 4), pl.ds(4, 4)

    def multiply(pair, first_row=0, last_row=8):
        left = [field[s, pair // 2].reshape(128, 192) for s in range(2)]

        def row(r, _):
            value = jnp.dot(left[0], ct[pair % 2, r, 0], preferred_element_type=F32)
            value = value + jnp.dot(left[1], ct[pair % 2, r, 1], preferred_element_type=F32)
            value = value.astype(BF16).reshape(2, 4, 2, 8, 640)
            for core in range(2):
                part[2 * pair + core, :, :, r] = value[core]
            return 0

        lax.fori_loop(first_row, last_row, row, 0)

    def multiply_z(h):
        left = [field[s, h, c] for s in range(2)]

        def row(r, _):
            value = jnp.dot(left[0], ct[2, r, 0], preferred_element_type=F32)
            value = value + jnp.dot(left[1], ct[2, r, 1], preferred_element_type=F32)
            part[8 + h, :, :, r] = value.astype(BF16).reshape(4, 2, 8, 640)
            return 0

        for rows in (low, high):
            lax.fori_loop(rows.start, rows.start + 4, row, 0)
            z_first(8 + h, rows).start()

    def z_first(k, rows):
        return remote(
            part.at[k, :, 1 - z, rows], zin.at[k - 8, :, rows], z_send, z_in.at[k - 8], to_z
        )

    def z_copy(k):
        return remote(z_out.at[k], from_z.at[k], z_send, last_in.at[k], to_z)

    def sum_z(k):
        settle(zin.at[k - 8], z_in.at[k - 8])
        total = part[k, :, z].astype(F32) + zin[k - 8].astype(F32)
        zsum[k - 8] = total.astype(BF16)

    def arrivals(k, step):
        return (far_in, near_in, near_in, last_in)[step].at[k]

    def send_up(k, step):
        if k >= 8:
            pair = (
                (zsum.at[k - 8, far, low], z_pass_up.at[k - 8]),
                (zsum.at[k - 8, up, high], z_from_down.at[k - 8, high]),
                (z_pass_up.at[k - 8], z_from_down.at[k - 8, low]),
            )[step]
        else:
            pair = (
                (part.at[k, far, :, low], pass_up.at[k]),
                (part.at[k, up, :, high], from_down.at[k, :, high]),
                (pass_up.at[k, 1 - z], from_down.at[k, 1 - z, low]),
                (pass_up.at[k, z], from_down.at[k, z, low]),
            )[step]
        return remote(pair[0], pair[1], y_send.at[k // 8], arrivals(k, step), to_up)

    def send_down(k, step):
        if k >= 8:
            pair = (
                (zsum.at[k - 8, far, high], z_pass_down.at[k - 8]),
                (zsum.at[k - 8, down, low], z_from_up.at[k - 8, low]),
                (z_pass_down.at[k - 8], z_from_up.at[k - 8, high]),
            )[step]
        else:
            pair = (
                (part.at[k, far, :, high], pass_down.at[k]),
                (part.at[k, down, :, low], from_up.at[k, :, low]),
                (pass_down.at[k, 1 - z], from_up.at[k, 1 - z, high]),
                (pass_down.at[k, z], from_up.at[k, z, high]),
            )[step]
        return remote(pair[0], pair[1], y_send.at[k // 8], arrivals(k, step), to_down)

    def begin(k, *which):
        for step in which or (0, 1):
            send_up(k, step).start()
            send_down(k, step).start()

    def pass_on(k):
        settle(z_from_down.at[k - 8] if k >= 8 else from_down.at[k], far_in.at[k])
        if k >= 8:
            total = z_pass_up[k - 8].astype(F32) + zsum[k - 8, up, 0:4].astype(F32)
            z_pass_up[k - 8] = total.astype(BF16)
            send_up(k, 2).start()
            total = z_pass_down[k - 8].astype(F32) + zsum[k - 8, down, 4:8].astype(F32)
            z_pass_down[k - 8] = total.astype(BF16)
            send_down(k, 2).start()
            return
        for zz, step in ((1 - z, 2), (z, 3)):
            total = pass_up[k, zz].astype(F32) + part[k, up, zz, 0:4].astype(F32)
            pass_up[k, zz] = total.astype(BF16)
            send_up(k, step).start()
            total = pass_down[k, zz].astype(F32) + part[k, down, zz, 4:8].astype(F32)
            pass_down[k, zz] = total.astype(BF16)
            send_down(k, step).start()

    def gathered(k):
        settle(from_down.at[0] if k >= 8 else pass_up.at[pl.ds(0, 3)], near_in.at[k])

    def over_z(k):
        gathered(k)
        other = 1 - z
        total = part[k, y, other].astype(F32) + from_down[k, other].astype(F32)
        z_out[k] = (total + from_up[k, other].astype(F32)).astype(BF16)
        z_copy(k).start()

    def group_of(k):
        return 4 if k >= 8 else 2 * c + (k // 2) % 2

    def core_of(k):
        return c if k >= 8 else k % 2

    def half_of(k):
        return k - 8 if k >= 8 else k // 4

    def owner_walk(k, i):
        to_x, to_zh, to_zl = owner(half_of(k), z, i)
        return to_x * 4 + to_zh, to_zl

    def owner_copy(k, i):
        group = group_of(k)
        walk, zl = owner_walk(k, i)
        return remote(
            turned.at[8 * k + i], operator.at[group, a], o_send, o_recv.at[group],
            at(walk, y, zl, core_of(k)),
        )

    def each_owner(k, other, own=None):
        def run(d, _):
            i = ((x + away(d % 4)) % 4) * 2 + 1 - d // 4
            here = jnp.logical_and(owner_walk(k, i)[0] == a, core_of(k) == c)

            @pl.when(jnp.logical_not(here))
            def _():
                other(i)

            if own is not None:

                @pl.when(here)
                def _():
                    own(i)

            return 0

        lax.fori_loop(0, 8, run, 0)

    def deliver(k):
        if k >= 8:
            gathered(k)
            total = zsum[k - 8, y].astype(F32) + z_from_down[k - 8].astype(F32)
            total = total + z_from_up[k - 8].astype(F32)
        else:
            settle(from_down.at[k], last_in.at[k])
            total = part[k, y, z].astype(F32) + from_down[k, z].astype(F32)
            total = total + from_up[k, z].astype(F32) + from_z[k].astype(F32)
        turned[8 * k : 8 * k + 8] = jnp.swapaxes(total, 0, 1).astype(BF16)

        def keep(i):
            operator[group_of(k), a] = turned[8 * k + i]

        each_owner(k, lambda i: owner_copy(k, i).start(), keep)

    settle(ct.at[:, :, 1 - c], ct_recv)
    field_arrived(0)
    multiply(0, 0, 4)
    send_up(0, 0).start()
    send_down(0, 1).start()
    multiply(0, 4, 8)
    send_down(0, 0).start()
    send_up(0, 1).start()
    begin(1)
    start_zh(1)
    multiply_z(0)
    multiply(1)
    pass_on(0)
    begin(2)
    start_back(1)
    pass_on(1)
    begin(3)
    shift(1)
    over_z(0)
    field_arrived(1)
    multiply_z(1)
    pass_on(2)
    multiply(2)
    begin(4)
    over_z(1)
    multiply(3)
    pass_on(3)
    begin(5)
    sum_z(8)
    by_half = [
        jnp.swapaxes(jnp.swapaxes(dj[h], 0, 1).reshape(16, 8, 192), 0, 1) for h in range(2)
    ]
    aux_out[...] = jnp.stack(by_half, axis=1).reshape(256, 192).T
    over_z(2)
    pass_on(4)
    begin(6)
    deliver(0)
    deliver(1)
    over_z(3)
    pass_on(5)
    begin(7)
    deliver(2)
    deliver(3)
    sum_z(9)
    over_z(4)
    pass_on(6)
    deliver(4)
    over_z(5)
    pass_on(7)
    begin(8)
    begin(9)
    deliver(5)
    over_z(6)
    over_z(7)
    pass_on(8)
    deliver(6)
    pass_on(9)
    deliver(7)
    deliver(8)
    deliver(9)

    settle(gsend.at[pl.ds(0, 15)], a_send)
    settle(ct.at[:, :, c], ct_send)
    settle(blocks.at[pl.ds(0, 15)], g_send)
    settle(pb.at[pl.ds(0, 6)], p_send)
    settle(pb.at[pl.ds(0, 6)], q_send)
    settle(pb.at[pl.ds(0, 6)], b_send)
    settle(field.at[0], f_send)
    settle(part.at[pl.ds(0, 6)], y_send.at[0])
    settle(pass_up.at[pl.ds(0, 6)], y_send.at[1])
    settle(from_down, z_send)

    def wait_group(group):
        core = c if group == 4 else group // 2

        @pl.when(core == c)
        def _():
            settle(operator.at[group, pl.ds(0, 15)], o_recv.at[group])

        @pl.when(core != c)
        def _():
            settle(operator.at[group], o_recv.at[group])

    start_low = wv[0].astype(BF16)
    for group in (0, 2, 1, 3, 4):
        wait_group(group)
        rows = operator[group].reshape(128, 640)
        value = jnp.dot(rows, start_low, preferred_element_type=F32)
        term1[:, group] = value.reshape(16, 8, 128)
    settle(turned.at[pl.ds(0, 77)], o_send)
    matrix = jnp.swapaxes(operator[...], 0, 1).reshape(640, 640)
    term = term1[...].reshape(640, 128)
    total = wv[0] + term
    for degree in range(2, 5):
        term = jnp.dot(matrix, term.astype(BF16), preferred_element_type=F32) * (1.0 / degree)
        total = total + term
    out[0] = total


def hand_over(walkers_in, aux_in, walkers_out, aux_out):
    walkers_out[...] = walkers_in[...]
    aux_out[...] = aux_in[...]


def shape(*dims, dtype=BF16):
    return jax.ShapeDtypeStruct(dims, dtype)


def room(*dims, dtype=BF16):
    return pltpu.VMEM(dims, dtype)


def dma(*dims):
    return pltpu.SemaphoreType.DMA(dims)


def body(walkers, intersection_inverse, aux_draws, chol_half, chol_full):
    new_walkers, aux = pl.pallas_call(
        kernel,
        out_shape=(shape(1, 640, 128, dtype=F32), shape(192, 256, dtype=F32)),
        in_specs=[ANY] * 5,
        out_specs=(VMEM, VMEM),
        scratch_shapes=[
            room(1, 640, 128, dtype=F32),
            room(1, 128, 128, dtype=F32),
            room(192, 256, dtype=F32),
            room(192, 40, 128),
            room(192, 40, 640),
            room(16, 40, 128),
            room(16, 2, 8, 40, 128),
            room(2, 40, 8, 16, 128),
            room(40, 192, 128),
            room(40, 128, 192),
            room(3, 8, 2, 192, 640),
            room(2, 8, 192, 640),
            room(2, 64, 64),
            room(2, 2, 8, 8, 192, dtype=F32),
            room(8, 32, 192),
            room(2, 4, 32, 192),
            room(2, 4, 32, 192),
            room(2, 4, 32, 192),
            room(2, 2, 2, 64, 192),
            room(10, 4, 2, 8, 8, 640),
            room(8, 2, 4, 8, 640),
            room(8, 2, 4, 8, 640),
            room(8, 2, 8, 8, 640),
            room(8, 2, 8, 8, 640),
            room(8, 8, 8, 640),
            room(8, 8, 8, 640),
            room(2, 4, 8, 8, 640),
            room(2, 4, 8, 8, 640),
            room(2, 4, 8, 640),
            room(2, 4, 8, 640),
            room(2, 8, 8, 640),
            room(2, 8, 8, 640),
            room(80, 8, 640),
            room(5, 16, 8, 640),
            room(16, 5, 8, 128, dtype=F32),
            dma(5), dma(), dma(), dma(), dma(2), dma(), dma(2, 8), dma(), dma(2), dma(), dma(2),
            dma(), dma(2), dma(), dma(2), dma(2), dma(10), dma(10), dma(8), dma(), dma(2), dma(), dma(5),
        ],
        compiler_params=pltpu.CompilerParams(
            collective_id=0, has_side_effects=True, vmem_limit_bytes=56 * 2**20
        ),
        name="propagate",
    )(walkers, intersection_inverse, aux_draws.T, chol_half, chol_full)
    new_walkers, aux = pl.pallas_call(
        hand_over,
        out_shape=(shape(1, 640, 128, dtype=F32), shape(192, 256, dtype=F32)),
        in_specs=[VMEM] * 2,
        out_specs=(VMEM, VMEM),
        name="hand_over",
    )(new_walkers, aux)
    return new_walkers, aux.T


def solution(mesh):
    placed = (
        P(("walk", "chol"), None, None),
        P(("walk", "chol"), None, None),
        P(None, "chol"),
        P("chol", "walk", None),
        P("chol", "walk", None),
    )
    return jax.shard_map(
        body,
        mesh=mesh,
        in_specs=placed,
        out_specs=(P(("walk", "chol"), None, None), P(None, "chol")),
        check_vma=False,
    )
```

```python
import jax
import jax.numpy as jnp
from jax import lax
from jax.experimental import pallas as pl
from jax.experimental.pallas import tpu as pltpu
from jax.sharding import PartitionSpec as P

MESH = pl.DeviceIdType.MESH
BF16 = jnp.bfloat16
F32 = jnp.float32
ANY = pl.BlockSpec(memory_space=pl.ANY)
VMEM = pl.BlockSpec(memory_space=pltpu.VMEM)


def place():
    a = lax.axis_index("walk")
    b = lax.axis_index("chol")
    return a, b // 4, (b // 2) % 2, b % 2


def at(a, y, z, c):
    return (a, y * 4 + z * 2 + c)


def remote(src, dst, send, recv, target):
    return pltpu.make_async_remote_copy(
        src_ref=src, dst_ref=dst, send_sem=send, recv_sem=recv, device_id=target, device_id_type=MESH
    )


def settle(ref, sem):
    a, y, z, c = place()
    remote(ref, ref, sem, sem, at(a, y, z, 1 - c)).wait_recv()


def greet(target):
    pl.semaphore_signal(pltpu.get_barrier_semaphore(), inc=1, device_id=target, device_id_type=MESH)


def kernel(
    walkers, inverse, draws, half, full,
    out, aux_out,
    wv, iv, dv, hv, fv, gsend, blocks, gt, ht, htk, ct, given, order, dj, pb, xin, zhin, ball, field,
    part, pass_up, pass_down, from_down, from_up, z_out, from_z,
    zin, zsum, z_pass_up, z_pass_down, z_from_down, z_from_up, turned, operator, term1,
    in_sem, ct_send, ct_recv, a_send, a_recv, g_send, g_recv, p_send, p_recv, q_send, q_recv,
    b_send, b_recv, f_send, f_recv, y_send, far_in, near_in, last_in, z_send, z_in, o_send, o_recv,
):
    a, y, z, c = place()
    x, zh = a // 4, a % 4
    up, down, far = (y + 1) % 4, (y + 3) % 4, (y + 2) % 4
    to_up, to_down, to_z = at(a, up, z, c), at(a, down, z, c), at(a, y, 1 - z, c)
    sibling = at(a, y, z, 1 - c)

    def load(index):
        pair = ((walkers, wv), (inverse, iv), (half, hv), (full, fv), (draws, dv))[index]
        return pltpu.make_async_copy(pair[0], pair[1], in_sem.at[index])

    def greet_walk(d, _):
        greet(at((a + d) % 16, y, z, c))
        return 0

    lax.fori_loop(1, 16, greet_walk, 0)

    def greet_senders(d, _):
        xx, core = d // 2, d % 2

        @pl.when(jnp.logical_or(xx != x, core != c))
        def _():
            greet(at(xx * 4 + zh, y, z, core))

        greet(at(xx * 4 + (zh + 2) % 4, y, 1 - z, core))
        greet(at(xx * 4 + (zh + 3) % 4, y, 1, core))
        greet(at(xx * 4 + (zh + 1) % 4, y, 0, core))
        return 0

    lax.fori_loop(0, 8, greet_senders, 0)
    to_far = at(a, far, z, c)
    for target in (to_far, to_up, to_down, to_z, sibling):
        greet(target)

    for index in range(5):
        load(index).start()

    load(0).wait()
    load(1).wait()
    green = jnp.dot(
        wv[0], iv[0], precision=lax.Precision.HIGHEST, preferred_element_type=F32
    ).astype(BF16)
    gsend[...] = green.reshape(16, 40, 128)
    pl.semaphore_wait(pltpu.get_barrier_semaphore(), 51)

    def each_other(step):
        def run(d, _):
            step(d)
            return 0

        lax.fori_loop(1, 16, run, 0)

    def away(n):
        return jnp.where(n < 2, 2 + n, 3 - n)

    def peer(d):
        n = d - 1
        return ((x + away(n % 4)) % 4) * 4 + (zh + away(n // 4)) % 4

    def slot(yy, zz):
        return c * 8 + yy * 2 + zz

    own = slot(y, z)

    def green_copy(to):
        return remote(
            gsend.at[to], blocks.at[own, a % 2, a // 2], a_send, a_recv.at[a % 2], at(to, y, z, c)
        )

    @pl.when(a % 2 == 0)
    def _():
        each_other(lambda d: green_copy(peer(d)).start())

    blocks[own, a % 2, a // 2] = gsend[a]

    load(2).wait()

    def turn_half(i, _):
        n0 = pl.multiple_of(i * 16, 16)
        ht[:, pl.ds(n0, 16), :] = jnp.swapaxes(hv[pl.ds(n0, 16)], 0, 1)
        return 0

    lax.fori_loop(0, 12, turn_half, 0)

    load(3).wait()

    def turn_full(group, target):
        def turn(i, _):
            n0 = pl.multiple_of(i * 16, 16)
            target[:, pl.ds(n0, 16), :] = jnp.swapaxes(
                fv[pl.ds(n0, 16), group * 8 : group * 8 + 8, :], 0, 1
            )
            return 0

        lax.fori_loop(0, 12, turn, 0)

    def turn_given(i):
        for core in range(2):

            @pl.when(c == core)
            def _(core=core):
                turn_full(2 * (1 - core) + i, given.at[i])

    def turn_kept(i):
        for core in range(2):

            @pl.when(c == core)
            def _(core=core):
                turn_full(2 * core + i, ct.at[i, :, core])

    def give(i):
        source = ct.at[2, :, c] if i == 2 else given.at[i]
        return remote(source, ct.at[i, :, c], ct_send, ct_recv, sibling)

    turn_given(0)
    give(0).start()
    turn_given(1)
    give(1).start()
    for core in range(2):

        @pl.when(c == core)
        def _(core=core):
            turn_full(4, ct.at[2, :, core])

    give(2).start()

    @pl.when(a % 2 == 1)
    def _():
        each_other(lambda d: green_copy(peer(d)).start())

    turn_kept(0)
    turn_kept(1)

    def owner(h, zl, i):
        same = 1 - (zh + h) % 2
        pick = i % 2
        to_zh = (zh + same * 2 * pick + (1 - same) * (3 - 2 * zl)) % 4
        return i // 2, to_zh, same * ((zl + pick) % 2) + (1 - same) * pick

    for h in range(2):
        row = lax.broadcasted_iota(jnp.int32, (64, 64), 0)
        column = lax.broadcasted_iota(jnp.int32, (64, 64), 1)
        to_x, to_zh, to_zl = owner(h, (row // 8) % 2, row % 8)
        source = (row // 16) * 16 + to_zl * 8 + to_x * 2 + to_zh // 2
        order[h] = jnp.where(source == column, 1.0, 0.0).astype(BF16)

    load(4).wait()
    by_walker = dv[...].T.reshape(8, 2, 16, 192)
    for h in range(2):
        half_draws = jnp.swapaxes(by_walker[:, h], 0, 1).reshape(8, 2, 8, 192)
        for core in range(2):
            dj[h, core] = half_draws[:, core]

    def wait_green(h):
        @pl.when(a % 2 == h)
        def _():
            settle(blocks.at[0, h, pl.ds(0, 7)], a_recv.at[h])

        @pl.when(a % 2 != h)
        def _():
            settle(blocks.at[0, h], a_recv.at[h])

    def spread(h, index):
        yy, zz, target = (
            (y, z, to_far), (y, z, to_up), (y, z, to_down), (y, z, to_z), (y, z, sibling),
            (y, 1 - z, to_up), (y, 1 - z, to_down), (far, z, to_z),
            (y, 1 - z, sibling), (far, z, sibling), (down, z, sibling), (up, z, sibling),
            (down, 1 - z, sibling), (up, 1 - z, sibling), (far, 1 - z, sibling),
        )[index]
        ref = blocks.at[slot(yy, zz), h]
        return remote(ref, ref, g_send, g_recv.at[h, index if index < 8 else 4], target)

    def start(h, *indices):
        for index in indices:
            spread(h, index).start()

    def landed(h, index):
        settle(blocks.at[0, h], g_recv.at[h, index])

    def spread_own(h):
        start(h, 3, 0, 1, 2, 4)

    def spread_second(h):
        landed(h, 3)
        start(h, 5, 6, 8)
        landed(h, 0)
        start(h, 7, 9)

    def spread_on(h):
        for index in (1, 2, 5, 6, 7):
            landed(h, index)
            start(h, {1: 10, 2: 11, 5: 12, 6: 13, 7: 14}[index])
        settle(blocks.at[pl.ds(0, 4)], g_recv.at[h, 4])

    def bias_sums(h):
        def turn(i, _):
            both = blocks[pl.ds(2 * i, 2), h].reshape(16, 40, 128)
            gt[h, :, i] = jnp.swapaxes(both, 0, 1)
            return 0

        lax.fori_loop(0, 8, turn, 0)

        def step(i, acc):
            p0 = i * 8
            left = jnp.concatenate([gt[h, p0 + q].reshape(128, 128) for q in range(8)], axis=1)
            right = htk[pl.ds(p0, 8)].reshape(1024, 192)
            return acc + jnp.dot(left, right, preferred_element_type=F32)

        partial = lax.fori_loop(0, 5, step, jnp.zeros((128, 192), F32))
        pb[4 * h : 4 * h + 4] = partial.astype(BF16).reshape(4, 32, 192)

    def x_peer(e):
        return (x + e) % 4

    def x_copy(h, e):
        return remote(
            pb.at[4 * h + x_peer(e)], xin.at[h, x], p_send, p_recv.at[h],
            at(x_peer(e) * 4 + zh, y, z, c),
        )

    def zh_copy(h, e):
        ref = zhin.at[h, zh]
        return remote(ref, ref, q_send, q_recv.at[h], at(x * 4 + (zh + e) % 4, y, z, c))

    def back_copy(h, e):
        ref = ball.at[h, x]
        return remote(ref, ref, b_send, b_recv.at[h], at(x_peer(e) * 4 + zh, y, z, c))

    def start_x(h):
        for e in (2, 1, 3):
            x_copy(h, e).start()
        xin[h, x] = pb[4 * h + x]

    def start_zh(h):
        settle(xin.at[h, pl.ds(0, 3)], p_recv.at[h])
        zhin[h, zh] = jnp.sum(xin[h].astype(F32), axis=0).astype(BF16)
        for e in (2, 1, 3):
            zh_copy(h, e).start()

    def start_back(h):
        settle(zhin.at[h, pl.ds(0, 3)], q_recv.at[h])
        ball[h, x] = jnp.sum(zhin[h].astype(F32), axis=0).astype(BF16)
        for e in (2, 1, 3):
            back_copy(h, e).start()

    def field_copy(h):
        ref = field.at[c, h]
        return remote(ref, ref, f_send, f_recv.at[h], sibling)

    def field_arrived(h):
        settle(field.at[0, h], f_recv.at[h])

    def shift(h):
        settle(ball.at[h, pl.ds(0, 3)], b_recv.at[h])
        shifted = dj[h] - ball[h].astype(F32).reshape(2, 8, 8, 192)
        dj[h] = shifted
        for core in range(2):
            rows = shifted[core].astype(BF16).reshape(64, 192)
            rows = jnp.dot(order[h], rows, preferred_element_type=F32)
            field[c, h, core] = rows.astype(BF16)
        field_copy(h).start()

    def turn_columns(i, _):
        for q in range(4):
            htk[4 * i + q] = ht[4 * i + q].astype(F32).T.astype(BF16)
        return 0

    wait_green(0)
    spread_own(0)
    lax.fori_loop(0, 5, turn_columns, 0)
    spread_second(0)
    wait_green(1)
    spread_own(1)
    lax.fori_loop(5, 10, turn_columns, 0)
    spread_on(0)
    bias_sums(0)
    start_x(0)
    spread_second(1)
    start_zh(0)
    spread_on(1)
    start_back(0)
    bias_sums(1)
    start_x(1)
    shift(0)

    low, high = pl.ds(0, 4), pl.ds(4, 4)

    def multiply(pair, first_row=0, last_row=8):
        left = [field[s, pair // 2].reshape(128, 192) for s in range(2)]

        def row(r, _):
            value = jnp.dot(left[0], ct[pair % 2, r, 0], preferred_element_type=F32)
            value = value + jnp.dot(left[1], ct[pair % 2, r, 1], preferred_element_type=F32)
            value = value.astype(BF16).reshape(2, 4, 2, 8, 640)
            for core in range(2):
                part[2 * pair + core, :, :, r] = value[core]
            return 0

        lax.fori_loop(first_row, last_row, row, 0)

    def multiply_z(h):
        left = [field[s, h, c] for s in range(2)]

        def row(r, _):
            value = jnp.dot(left[0], ct[2, r, 0], preferred_element_type=F32)
            value = value + jnp.dot(left[1], ct[2, r, 1], preferred_element_type=F32)
            part[8 + h, :, :, r] = value.astype(BF16).reshape(4, 2, 8, 640)
            return 0

        for rows in (low, high):
            lax.fori_loop(rows.start, rows.start + 4, row, 0)
            z_first(8 + h, rows).start()

    def z_first(k, rows):
        return remote(
            part.at[k, :, 1 - z, rows], zin.at[k - 8, :, rows], z_send, z_in.at[k - 8], to_z
        )

    def z_copy(k):
        return remote(z_out.at[k], from_z.at[k], z_send, last_in.at[k], to_z)

    def sum_z(k):
        settle(zin.at[k - 8], z_in.at[k - 8])
        total = part[k, :, z].astype(F32) + zin[k - 8].astype(F32)
        zsum[k - 8] = total.astype(BF16)

    def arrivals(k, step):
        return (far_in, near_in, near_in, last_in)[step].at[k]

    def send_up(k, step):
        if k >= 8:
            pair = (
                (zsum.at[k - 8, far, low], z_pass_up.at[k - 8]),
                (zsum.at[k - 8, up, high], z_from_down.at[k - 8, high]),
                (z_pass_up.at[k - 8], z_from_down.at[k - 8, low]),
            )[step]
        else:
            pair = (
                (part.at[k, far, :, low], pass_up.at[k]),
                (part.at[k, up, :, high], from_down.at[k, :, high]),
                (pass_up.at[k, 1 - z], from_down.at[k, 1 - z, low]),
                (pass_up.at[k, z], from_down.at[k, z, low]),
            )[step]
        return remote(pair[0], pair[1], y_send.at[k // 8], arrivals(k, step), to_up)

    def send_down(k, step):
        if k >= 8:
            pair = (
                (zsum.at[k - 8, far, high], z_pass_down.at[k - 8]),
                (zsum.at[k - 8, down, low], z_from_up.at[k - 8, low]),
                (z_pass_down.at[k - 8], z_from_up.at[k - 8, high]),
            )[step]
        else:
            pair = (
                (part.at[k, far, :, high], pass_down.at[k]),
                (part.at[k, down, :, low], from_up.at[k, :, low]),
                (pass_down.at[k, 1 - z], from_up.at[k, 1 - z, high]),
                (pass_down.at[k, z], from_up.at[k, z, high]),
            )[step]
        return remote(pair[0], pair[1], y_send.at[k // 8], arrivals(k, step), to_down)

    def begin(k, *which):
        for step in which or (0, 1):
            send_up(k, step).start()
            send_down(k, step).start()

    def pass_on(k):
        settle(z_from_down.at[k - 8] if k >= 8 else from_down.at[k], far_in.at[k])
        if k >= 8:
            total = z_pass_up[k - 8].astype(F32) + zsum[k - 8, up, 0:4].astype(F32)
            z_pass_up[k - 8] = total.astype(BF16)
            send_up(k, 2).start()
            total = z_pass_down[k - 8].astype(F32) + zsum[k - 8, down, 4:8].astype(F32)
            z_pass_down[k - 8] = total.astype(BF16)
            send_down(k, 2).start()
            return
        for zz, step in ((1 - z, 2), (z, 3)):
            total = pass_up[k, zz].astype(F32) + part[k, up, zz, 0:4].astype(F32)
            pass_up[k, zz] = total.astype(BF16)
            send_up(k, step).start()
            total = pass_down[k, zz].astype(F32) + part[k, down, zz, 4:8].astype(F32)
            pass_down[k, zz] = total.astype(BF16)
            send_down(k, step).start()

    def gathered(k):
        settle(from_down.at[0] if k >= 8 else pass_up.at[pl.ds(0, 3)], near_in.at[k])

    def over_z(k):
        gathered(k)
        other = 1 - z
        total = part[k, y, other].astype(F32) + from_down[k, other].astype(F32)
        z_out[k] = (total + from_up[k, other].astype(F32)).astype(BF16)
        z_copy(k).start()

    def group_of(k):
        return 4 if k >= 8 else 2 * c + (k // 2) % 2

    def core_of(k):
        return c if k >= 8 else k % 2

    def half_of(k):
        return k - 8 if k >= 8 else k // 4

    def owner_walk(k, i):
        to_x, to_zh, to_zl = owner(half_of(k), z, i)
        return to_x * 4 + to_zh, to_zl

    def owner_copy(k, i):
        group = group_of(k)
        walk, zl = owner_walk(k, i)
        return remote(
            turned.at[8 * k + i], operator.at[group, a], o_send, o_recv.at[group],
            at(walk, y, zl, core_of(k)),
        )

    def each_owner(k, other, own=None):
        def run(d, _):
            i = ((x + away(d % 4)) % 4) * 2 + 1 - d // 4
            here = jnp.logical_and(owner_walk(k, i)[0] == a, core_of(k) == c)

            @pl.when(jnp.logical_not(here))
            def _():
                other(i)

            if own is not None:

                @pl.when(here)
                def _():
                    own(i)

            return 0

        lax.fori_loop(0, 8, run, 0)

    def deliver(k):
        if k >= 8:
            gathered(k)
            total = zsum[k - 8, y].astype(F32) + z_from_down[k - 8].astype(F32)
            total = total + z_from_up[k - 8].astype(F32)
        else:
            settle(from_down.at[k], last_in.at[k])
            total = part[k, y, z].astype(F32) + from_down[k, z].astype(F32)
            total = total + from_up[k, z].astype(F32) + from_z[k].astype(F32)
        turned[8 * k : 8 * k + 8] = jnp.swapaxes(total, 0, 1).astype(BF16)

        def keep(i):
            operator[group_of(k), a] = turned[8 * k + i]

        each_owner(k, lambda i: owner_copy(k, i).start(), keep)

    settle(ct.at[:, :, 1 - c], ct_recv)
    field_arrived(0)
    multiply(0, 0, 4)
    send_up(0, 0).start()
    send_down(0, 1).start()
    multiply(0, 4, 8)
    send_down(0, 0).start()
    send_up(0, 1).start()
    begin(1)
    start_zh(1)
    multiply_z(0)
    multiply(1)
    pass_on(0)
    begin(2)
    start_back(1)
    pass_on(1)
    begin(3)
    shift(1)
    over_z(0)
    field_arrived(1)
    multiply_z(1)
    pass_on(2)
    multiply(2)
    begin(4)
    over_z(1)
    multiply(3)
    pass_on(3)
    begin(5)
    sum_z(8)
    by_half = [
        jnp.swapaxes(jnp.swapaxes(dj[h], 0, 1).reshape(16, 8, 192), 0, 1) for h in range(2)
    ]
    aux_out[...] = jnp.stack(by_half, axis=1).reshape(256, 192).T
    over_z(2)
    pass_on(4)
    begin(6)
    deliver(0)
    deliver(1)
    over_z(3)
    pass_on(5)
    begin(7)
    deliver(2)
    deliver(3)
    sum_z(9)
    over_z(4)
    pass_on(6)
    deliver(4)
    over_z(5)
    pass_on(7)
    begin(8)
    begin(9)
    deliver(5)
    over_z(6)
    over_z(7)
    pass_on(8)
    deliver(6)
    pass_on(9)
    deliver(7)
    deliver(8)
    deliver(9)

    settle(gsend.at[pl.ds(0, 15)], a_send)
    settle(ct.at[:, :, c], ct_send)
    settle(blocks.at[pl.ds(0, 15)], g_send)
    settle(pb.at[pl.ds(0, 6)], p_send)
    settle(pb.at[pl.ds(0, 6)], q_send)
    settle(pb.at[pl.ds(0, 6)], b_send)
    settle(field.at[0], f_send)
    settle(part.at[pl.ds(0, 6)], y_send.at[0])
    settle(pass_up.at[pl.ds(0, 6)], y_send.at[1])
    settle(from_down, z_send)

    def wait_group(group):
        core = c if group == 4 else group // 2

        @pl.when(core == c)
        def _():
            settle(operator.at[group, pl.ds(0, 15)], o_recv.at[group])

        @pl.when(core != c)
        def _():
            settle(operator.at[group], o_recv.at[group])

    start_low = wv[0].astype(BF16)
    for group in (0, 2, 1, 3, 4):
        wait_group(group)
        rows = operator[group].reshape(128, 640)
        value = jnp.dot(rows, start_low, preferred_element_type=F32)
        term1[:, group] = value.reshape(16, 8, 128)
    settle(turned.at[pl.ds(0, 77)], o_send)
    matrix = jnp.swapaxes(operator[...], 0, 1).reshape(640, 640)
    term = term1[...].reshape(640, 128)
    out[0] = wv[0] + term
    low_term = term.astype(BF16)
    for degree in range(2, 5):
        pieces = []
        for first_row in range(0, 640, 128):
            rows = matrix[first_row : first_row + 128]
            value = jnp.dot(rows, low_term, preferred_element_type=F32) * (1.0 / degree)
            out[0, first_row : first_row + 128] += value
            pieces.append(value.astype(BF16))
        low_term = jnp.concatenate(pieces, axis=0)


def hand_over(walkers_in, aux_in, walkers_out, aux_out):
    walkers_out[...] = walkers_in[...]
    aux_out[...] = aux_in[...]


def shape(*dims, dtype=BF16):
    return jax.ShapeDtypeStruct(dims, dtype)


def room(*dims, dtype=BF16):
    return pltpu.VMEM(dims, dtype)


def dma(*dims):
    return pltpu.SemaphoreType.DMA(dims)


def body(walkers, intersection_inverse, aux_draws, chol_half, chol_full):
    new_walkers, aux = pl.pallas_call(
        kernel,
        out_shape=(shape(1, 640, 128, dtype=F32), shape(192, 256, dtype=F32)),
        in_specs=[ANY] * 5,
        out_specs=(VMEM, VMEM),
        scratch_shapes=[
            room(1, 640, 128, dtype=F32),
            room(1, 128, 128, dtype=F32),
            room(192, 256, dtype=F32),
            room(192, 40, 128),
            room(192, 40, 640),
            room(16, 40, 128),
            room(16, 2, 8, 40, 128),
            room(2, 40, 8, 16, 128),
            room(40, 192, 128),
            room(40, 128, 192),
            room(3, 8, 2, 192, 640),
            room(2, 8, 192, 640),
            room(2, 64, 64),
            room(2, 2, 8, 8, 192, dtype=F32),
            room(8, 32, 192),
            room(2, 4, 32, 192),
            room(2, 4, 32, 192),
            room(2, 4, 32, 192),
            room(2, 2, 2, 64, 192),
            room(10, 4, 2, 8, 8, 640),
            room(8, 2, 4, 8, 640),
            room(8, 2, 4, 8, 640),
            room(8, 2, 8, 8, 640),
            room(8, 2, 8, 8, 640),
            room(8, 8, 8, 640),
            room(8, 8, 8, 640),
            room(2, 4, 8, 8, 640),
            room(2, 4, 8, 8, 640),
            room(2, 4, 8, 640),
            room(2, 4, 8, 640),
            room(2, 8, 8, 640),
            room(2, 8, 8, 640),
            room(80, 8, 640),
            room(5, 16, 8, 640),
            room(16, 5, 8, 128, dtype=F32),
            dma(5), dma(), dma(), dma(), dma(2), dma(), dma(2, 8), dma(), dma(2), dma(), dma(2),
            dma(), dma(2), dma(), dma(2), dma(2), dma(10), dma(10), dma(8), dma(), dma(2), dma(), dma(5),
        ],
        compiler_params=pltpu.CompilerParams(
            collective_id=0, has_side_effects=True, vmem_limit_bytes=56 * 2**20
        ),
        name="propagate",
    )(walkers, intersection_inverse, aux_draws.T, chol_half, chol_full)
    new_walkers, aux = pl.pallas_call(
        hand_over,
        out_shape=(shape(1, 640, 128, dtype=F32), shape(192, 256, dtype=F32)),
        in_specs=[VMEM] * 2,
        out_specs=(VMEM, VMEM),
        name="hand_over",
    )(new_walkers, aux)
    return new_walkers, aux.T


def solution(mesh):
    placed = (
        P(("walk", "chol"), None, None),
        P(("walk", "chol"), None, None),
        P(None, "chol"),
        P("chol", "walk", None),
        P("chol", "walk", None),
    )
    return jax.shard_map(
        body,
        mesh=mesh,
        in_specs=placed,
        out_specs=(P(("walk", "chol"), None, None), P(None, "chol")),
        check_vma=False,
    )
```
